32 devices in a mesh: group: 2 (over y), layout: 4 (over z), kernel: 4 (over x, core).
Axes of the slice: x: 2, y: 2, z: 4, core: 2. Of those that a mesh axis runs over, the one named last changes fastest.
Arguments:
- theta: bfloat16 [2048, 512], P(('group', 'layout')), parts along dimension 0, may hold values from -6 to 6
- target: bfloat16 [2048, 512], P(('group', 'layout')), parts along dimension 0, may hold values from 0 to 1
- occupancy: int32 [8, 2], P(('group', 'layout')), parts along dimension 0, may hold values from 0 to 1, as said below
- kernels: bfloat16 [2, 8, 19, 19], P(None, 'kernel'), may hold values from -0.3125 to 0.3125
- kernel_weights: float32 [8], P('kernel'), may hold values from 0.04 to 0.4
Outputs:
- mask_gradient: float32 [2048, 512], P(('group', 'layout', 'kernel')), parts along dimension 0
The draws below stay inside these ranges and needn't reach their ends.
There are 2 independent parts, one for each index of `group`. The reference program is written for one: setup_inputs(seed, part) draws one part's arguments, and reference() takes and returns one part's arrays. A program takes and returns all parts, laid end to end along the dimension named above; an argument that names none is the same for every part. Nothing has to cross between parts.
Inputs may be any that keep to these rules, and one draw needn't show every extreme that they name: `occupancy`: 1 marks a tile that holds layout, 0 an empty tile; exactly 4 tiles of the map are marked 1.
All inputs are finite; a program needn't handle non-finite values.
Results may differ from the reference program's by a relative error of at most 0.0065.
Values may be sent and summed in bfloat16 or wider, within the bound.
A program may use at most 128 MiB of HBM per device.

```python
import math
import jax
import jax.numpy as jnp
from jax import lax

TILE = 256
KSIZE = 19
ROWS = 2
KERNELS = 8
NX = 1024
NY = 512
N_LAYOUT = 4


def draw_occupancy(key, part):
    key = jax.random.fold_in(key, 11)
    tile_total = N_LAYOUT * ROWS
    order = jax.random.permutation(key, tile_total)
    marked = (order < tile_total // 2).astype(jnp.int32)
    return marked.reshape(N_LAYOUT, ROWS)


def shard_levels(own_key, shape, cuts, least, top_value):
    gain = 1.0
    for axis_at, blocks in cuts:
        draws = jax.random.uniform(jax.random.fold_in(jax.random.fold_in(own_key, 6), axis_at), (blocks,), jnp.float32, least / len(cuts), top_value / len(cuts))
        gain = gain * jnp.repeat(jnp.exp(draws), shape[axis_at] // blocks).reshape((-1,) + (1,) * (len(shape) - 1 - axis_at))
    return gain


def bell_draw(stream_key, extent, spread, limit, cuts=(), kind=jnp.bfloat16):
    array = spread * jax.random.normal(stream_key, extent, jnp.float32)
    if cuts:
        array = array * shard_levels(stream_key, extent, cuts, -0.22, 0.18)
    return jnp.clip(array, -limit, limit).astype(kind)


def setup_inputs(seed: int = 0, part: int = 0) -> dict:
    seeds = jax.random.split(jax.random.key(seed), 6)
    part_keys = jax.random.split(jax.random.fold_in(seeds[5], part), 6)
    return {
        "theta": bell_draw(part_keys[0], (NX, NY), 1.5, 6.0, ((0, 4),)),
        "target": jnp.clip(1.0 * jax.random.uniform(part_keys[1], (NX, NY), jnp.float32) ** shard_levels(part_keys[1], (NX, NY), ((0, 4),), -0.2, 0.2), 0.0, 1.0).astype(jnp.bfloat16),
        "occupancy": draw_occupancy(jax.random.fold_in(jax.random.fold_in(seeds[5], part), 71), part),
        "kernels": bell_draw(seeds[3], (2, KERNELS, KSIZE, KSIZE), (KSIZE * KSIZE) ** -0.5, 0.3125, ((1, 4),)),
        "kernel_weights": jnp.clip(jnp.exp(math.log(0.4) - 2.3025851 * jax.random.uniform(seeds[4], (KERNELS,), jnp.float32) ** shard_levels(seeds[4], (KERNELS,), ((0, 4),), -0.2, 0.2)), 0.04, 0.4),
    }


steepness = 8.0
threshold = 1.0


def correlate(image_hat, kernel_taps, size_x, size_y, radius, image_rows, image_cols):
    taps_hat = jnp.fft.rfft2(kernel_taps[::-1, ::-1], s=(size_x, size_y))
    whole = jnp.fft.irfft2(image_hat * taps_hat, s=(size_x, size_y))
    return whole[radius:radius + image_rows, radius:radius + image_cols]


def convolve(image, kernel_taps, size_x, size_y, radius, image_rows, image_cols):
    image_hat = jnp.fft.rfft2(image, s=(size_x, size_y))
    taps_hat = jnp.fft.rfft2(kernel_taps, s=(size_x, size_y))
    whole = jnp.fft.irfft2(image_hat * taps_hat, s=(size_x, size_y))
    return whole[radius:radius + image_rows, radius:radius + image_cols]


def reference(theta, target, occupancy, kernels, kernel_weights):
    image_rows, image_cols = theta.shape
    radius = KSIZE // 2
    size_x = image_rows + 2 * KSIZE
    size_y = image_cols + 2 * KSIZE
    live_pixels = jnp.repeat(jnp.repeat(occupancy.astype(jnp.float32), TILE, axis=0), TILE, axis=1)
    sigmoid_theta = jax.nn.sigmoid(theta.astype(jnp.float32))
    mask_values = lax.optimization_barrier((sigmoid_theta * live_pixels).astype(jnp.bfloat16)).astype(jnp.float32)
    mask_hat = jnp.fft.rfft2(mask_values, s=(size_x, size_y))
    kernel_taps = kernels.astype(jnp.float32)

    def field_pair(kernel_index):
        real_part = correlate(mask_hat, kernel_taps[0, kernel_index], size_x, size_y, radius, image_rows, image_cols)
        imag_part = correlate(mask_hat, kernel_taps[1, kernel_index], size_x, size_y, radius, image_rows, image_cols)
        return real_part, imag_part

    def add_intensity(running, kernel_index):
        real_part, imag_part = field_pair(kernel_index)
        return running + kernel_weights[kernel_index] * (real_part * real_part + imag_part * imag_part), None

    indices = jnp.arange(KERNELS, dtype=jnp.int32)
    intensity, _ = lax.scan(add_intensity, jnp.zeros((image_rows, image_cols), jnp.float32), indices)
    resist = jax.nn.sigmoid(steepness * (intensity - threshold))
    response = 2.0 * steepness * (resist - target.astype(jnp.float32)) * resist * (1.0 - resist) * live_pixels

    def add_gradient(running, kernel_index):
        real_part, imag_part = field_pair(kernel_index)
        factor = 2.0 * kernel_weights[kernel_index] * response
        real_product = lax.optimization_barrier((factor * real_part).astype(jnp.bfloat16)).astype(jnp.float32)
        imag_product = lax.optimization_barrier((factor * imag_part).astype(jnp.bfloat16)).astype(jnp.float32)
        back = convolve(real_product, kernel_taps[0, kernel_index], size_x, size_y, radius, image_rows, image_cols)
        back = back + convolve(imag_product, kernel_taps[1, kernel_index], size_x, size_y, radius, image_rows, image_cols)
        return running + back, None

    gradient, _ = lax.scan(add_gradient, jnp.zeros((image_rows, image_cols), jnp.float32), indices)
    return gradient * live_pixels
```

```python
import functools
import jax
import jax.numpy as jnp
from jax import lax
from jax.experimental import pallas as pl
from jax.experimental.pallas import tpu as pltpu
from jax.sharding import PartitionSpec as P

steepness = 8.0
threshold = 1.0
step_rows = 16
margin = 16
halo_rows = 32
tap_rows = 24
mesh_id = pl.DeviceIdType.MESH


def band_kernel(
    layouts, sharers, theta_ref, target_ref, occupancy_ref, kernels_ref, weights_ref, out_ref,
    gathered, halo_out, halo_in, mask_ref, target_near, live_near, shifted, products, forward_ref,
    adjoint_ref, send_sem, recv_sem, halo_send_sem, halo_recv_sem,
):
    local_rows, cols = theta_ref.shape
    parts, own_kernels, edge, _ = kernels_ref.shape
    own_channels = parts * own_kernels
    channels = own_channels * sharers
    radius = edge // 2
    share = local_rows // sharers
    lanes = mask_ref.shape[1]
    forward_window = (shifted.shape[1] - (share + 2 * margin)) + step_rows
    forward_depth = forward_ref.shape[1]
    adjoint_window = step_rows + 2 * margin
    adjoint_depth = adjoint_ref.shape[1]
    column = lax.axis_index("layout")
    sharer = lax.axis_index("kernel")
    is_first = sharer == 0
    is_last = sharer == sharers - 1
    has_low = jnp.logical_and(is_first, column > 0)
    has_high = jnp.logical_and(is_last, column < layouts - 1)
    sends_up = jnp.logical_and(is_first, column < layouts - 1)
    sends_down = jnp.logical_and(is_last, column > 0)
    at_edge = jnp.logical_or(is_first, is_last)

    barrier = pltpu.get_barrier_semaphore()
    for offset in range(1, sharers):
        pl.semaphore_signal(
            barrier, inc=1, device_id={"kernel": lax.rem(sharer + offset, sharers)},
            device_id_type=mesh_id,
        )

    @pl.when(jnp.logical_and(at_edge, column > 0))
    def _():
        pl.semaphore_signal(
            barrier, inc=1, device_id={"layout": column - 1}, device_id_type=mesh_id
        )

    @pl.when(jnp.logical_and(at_edge, column < layouts - 1))
    def _():
        pl.semaphore_signal(
            barrier, inc=1, device_id={"layout": column + 1}, device_id_type=mesh_id
        )

    gathered[0] = jnp.zeros(gathered.shape[1:], jnp.float32)
    for channel in range(own_channels):
        gathered[0, channel * tap_rows : channel * tap_rows + edge, 0:edge] = kernels_ref[
            channel // own_kernels, channel % own_kernels
        ].astype(jnp.float32)
        gathered[0, own_channels * tap_rows + channel, :] = jnp.full(
            (128,), weights_ref[channel % own_kernels], jnp.float32
        )

    tile_edge = cols // occupancy_ref.shape[1]
    lane = lax.broadcasted_iota(jnp.int32, (1, cols), 1)
    live_line = jnp.zeros((1, cols), jnp.float32)
    for tile in range(occupancy_ref.shape[1]):
        inside = jnp.logical_and(lane >= tile * tile_edge, lane < (tile + 1) * tile_edge)
        live_line = jnp.where(inside, occupancy_ref[0, tile].astype(jnp.float32), live_line)

    def mask_of(start, count):
        values = jax.nn.sigmoid(theta_ref[pl.ds(start, count), :].astype(jnp.float32)) * live_line
        return values.astype(jnp.bfloat16)

    def fill_halo(theta_start, target_start):
        halo_out[0:halo_rows, :] = mask_of(theta_start, halo_rows)
        halo_out[halo_rows : halo_rows + margin, :] = target_ref[pl.ds(target_start, margin), :]
        halo_out[halo_rows + margin :, :] = jnp.broadcast_to(live_line, (margin, cols)).astype(
            jnp.bfloat16
        )

    @pl.when(sends_up)
    def _():
        fill_halo(local_rows - halo_rows, local_rows - margin)

    @pl.when(sends_down)
    def _():
        fill_halo(0, 0)

    greeted = (column > 0).astype(jnp.int32) + (column < layouts - 1).astype(jnp.int32)
    pl.semaphore_wait(barrier, sharers - 1 + at_edge.astype(jnp.int32) * greeted)

    def halo_copy(side, neighbour):
        return pltpu.make_async_remote_copy(
            src_ref=halo_out, dst_ref=halo_in.at[side], send_sem=halo_send_sem,
            recv_sem=halo_recv_sem.at[side], device_id={"layout": neighbour},
            device_id_type=mesh_id,
        )

    @pl.when(sends_up)
    def _():
        halo_copy(0, column + 1).start()

    @pl.when(sends_down)
    def _():
        halo_copy(1, column - 1).start()

    tap_copies = [
        pltpu.make_async_remote_copy(
            src_ref=gathered.at[0], dst_ref=gathered.at[offset], send_sem=send_sem.at[offset],
            recv_sem=recv_sem.at[offset],
            device_id={"kernel": lax.rem(sharer + offset, sharers)}, device_id_type=mesh_id,
        )
        for offset in range(1, sharers)
    ]
    for copy in tap_copies:
        copy.start()

    first = pl.multiple_of(sharer * share, 32)
    mask_ref[:, cols:] = jnp.zeros((share + 2 * halo_rows, lanes - cols), jnp.float32)
    mask_ref[halo_rows : halo_rows + share, :cols] = mask_of(first, share).astype(jnp.float32)
    target_near[margin : margin + share, :] = target_ref[pl.ds(first, share), :].astype(
        jnp.float32
    )
    live_near[margin : margin + share, :] = jnp.broadcast_to(live_line, (share, cols))

    def place(mask_at, near_at, mask_values, target_values, live_values):
        mask_ref[mask_at : mask_at + halo_rows, :cols] = mask_values
        target_near[near_at : near_at + margin, :] = target_values
        live_near[near_at : near_at + margin, :] = live_values

    def place_own(mask_at, near_at, mask_start, near_start):
        place(
            mask_at, near_at, mask_of(mask_start, halo_rows).astype(jnp.float32),
            target_ref[pl.ds(near_start, margin), :].astype(jnp.float32),
            jnp.broadcast_to(live_line, (margin, cols)),
        )

    def place_received(mask_at, near_at, side):
        place(
            mask_at, near_at, halo_in[side, 0:halo_rows, :].astype(jnp.float32),
            halo_in[side, halo_rows : halo_rows + margin, :].astype(jnp.float32),
            halo_in[side, halo_rows + margin :, :].astype(jnp.float32),
        )

    def place_nothing(mask_at, near_at):
        place(
            mask_at, near_at, jnp.zeros((halo_rows, cols), jnp.float32),
            jnp.zeros((margin, cols), jnp.float32), jnp.zeros((margin, cols), jnp.float32),
        )

    high_mask, high_near = halo_rows + share, margin + share

    @pl.when(jnp.logical_not(is_first))
    def _():
        place_own(
            0, 0, pl.multiple_of(first - halo_rows, 32), pl.multiple_of(first - margin, 16)
        )

    @pl.when(jnp.logical_not(is_last))
    def _():
        after = pl.multiple_of(first + share, 32)
        place_own(high_mask, high_near, after, after)

    @pl.when(jnp.logical_and(is_first, column == 0))
    def _():
        place_nothing(0, 0)

    @pl.when(jnp.logical_and(is_last, column == layouts - 1))
    def _():
        place_nothing(high_mask, high_near)

    @pl.when(has_low)
    def _():
        halo_copy(0, column - 1).wait_recv()
        place_received(0, 0, 0)

    @pl.when(has_high)
    def _():
        halo_copy(1, column + 1).wait_recv()
        place_received(high_mask, high_near, 1)

    skip = halo_rows - margin - radius
    around = mask_ref[skip : skip + shifted.shape[1], :]
    for tap in range(edge):
        moved = around if tap == radius else pltpu.roll(around, (radius - tap) % lanes, 1)
        shifted[tap] = moved[:, :cols]

    for copy in tap_copies:
        copy.wait()

    taps = gathered[:, 0 : own_channels * tap_rows, :].reshape(channels * tap_rows, 128)
    taps = taps.astype(jnp.bfloat16)
    spread_row = lax.broadcasted_iota(jnp.int32, (128, forward_depth), 0)
    spread_lane = lax.broadcasted_iota(jnp.int32, (128, forward_depth), 1)
    ahead = spread_lane - forward_window * spread_row
    spread = jnp.logical_and(ahead >= 0, ahead < forward_window)
    spread = jnp.where(spread, 1.0, 0.0).astype(jnp.bfloat16)
    wide = jnp.dot(taps, spread, preferred_element_type=jnp.float32)
    wide = wide.reshape(channels, tap_rows, forward_depth)
    line = lax.broadcasted_iota(jnp.int32, (tap_rows, forward_depth), 1)
    down = lax.broadcasted_iota(jnp.int32, (tap_rows, forward_depth), 0)
    chosen = jnp.zeros((tap_rows, forward_depth), jnp.bool_)
    for tap in range(edge):
        chosen = jnp.logical_or(chosen, line - forward_window * tap == down)
    forward_line = jnp.sum(jnp.where(chosen[None], wide, 0.0), axis=1)

    def toeplitz(lines):
        count, depth = lines.shape
        rows = jnp.broadcast_to(lines[:, None, :], (count, step_rows, depth))
        rows = rows.reshape(count * step_rows, depth)
        place_in_step = lax.broadcasted_iota(jnp.int32, rows.shape, 0) & (step_rows - 1)
        bit = 1
        while bit < step_rows:
            rows = jnp.where((place_in_step & bit) != 0, pltpu.roll(rows, bit, 1), rows)
            bit *= 2
        return rows.astype(jnp.bfloat16)

    forward_ref[...] = toeplitz(forward_line)
    extent = (channels, tap_rows, adjoint_depth)
    channel_at = lax.broadcasted_iota(jnp.int32, extent, 0)
    row_at = lax.broadcasted_iota(jnp.int32, extent, 1)
    lane_at = lax.broadcasted_iota(jnp.int32, extent, 2)
    turn = lane_at == channel_at * adjoint_window + (margin + radius) - row_at
    turn = jnp.logical_and(turn, row_at < edge)
    turn = jnp.where(turn, 1.0, 0.0).reshape(channels * tap_rows, adjoint_depth)
    adjoint_line = lax.dot_general(
        taps, turn.astype(jnp.bfloat16), (((0,), (0,)), ((), ())),
        preferred_element_type=jnp.float32,
    )
    adjoint_ref[...] = toeplitz(adjoint_line[:edge])

    def weight_of(channel):
        slot, own = channel // own_channels, channel % own_channels
        at = own_channels * tap_rows + own
        return jnp.broadcast_to(gathered[slot, at : at + 1, 0:1], (step_rows, cols))

    pad_depth = forward_depth - edge * forward_window

    def forward_step(index):
        start = index * step_rows
        windows = shifted[:, pl.ds(start, forward_window), :].reshape(-1, cols)
        windows = jnp.concatenate([windows, jnp.zeros((pad_depth, cols), jnp.float32)], axis=0)
        fields = jnp.dot(
            forward_ref[...], windows.astype(jnp.bfloat16), preferred_element_type=jnp.float32
        ).reshape(channels, step_rows, cols)
        intensity = jnp.zeros((step_rows, cols), jnp.float32)
        for channel in range(channels):
            intensity += weight_of(channel) * (fields[channel] * fields[channel])
        resist = jax.nn.sigmoid(steepness * (intensity - threshold))
        response = 2.0 * steepness * (resist - target_near[pl.ds(start, step_rows), :])
        response = response * resist * (1.0 - resist) * live_near[pl.ds(start, step_rows), :]
        for channel in range(channels):
            factor = 2.0 * weight_of(channel) * response
            products[channel, pl.ds(start, step_rows), :] = (factor * fields[channel]).astype(
                jnp.bfloat16
            )

    def adjoint_step(index):
        start = index * step_rows
        windows = products[:, pl.ds(start, adjoint_window), :].reshape(-1, cols)
        terms = jnp.dot(adjoint_ref[...], windows, preferred_element_type=jnp.float32)
        beside = jnp.zeros((step_rows, lanes - cols), jnp.float32)
        total = terms[radius * step_rows : (radius + 1) * step_rows, :]
        for tap in range(edge):
            if tap != radius:
                term = terms[tap * step_rows : (tap + 1) * step_rows, :]
                term = jnp.concatenate([term, beside], axis=1)
                total = total + pltpu.roll(term, (tap - radius) % lanes, 1)[:, :cols]
        out_ref[pl.ds(start, step_rows), :] = total * live_line

    for index in range((share + 2 * margin) // step_rows):
        forward_step(index)
    for index in range(share // step_rows):
        adjoint_step(index)

    @pl.when(sends_up)
    def _():
        halo_copy(0, column + 1).wait_send()

    @pl.when(sends_down)
    def _():
        halo_copy(1, column - 1).wait_send()


def on_device(theta, target, occupancy, kernels, kernel_weights):
    local_rows, cols = theta.shape
    layouts, sharers = lax.axis_size("layout"), lax.axis_size("kernel")
    own_channels = kernels.shape[0] * kernels.shape[1]
    channels = own_channels * sharers
    edge = kernels.shape[-1]
    share = local_rows // sharers
    lanes = cols + 128
    forward_window = -(-(step_rows + edge - 1) // 8) * 8
    forward_depth = -(-edge * forward_window // 128) * 128
    adjoint_window = step_rows + 2 * margin
    near_rows = share + 2 * margin
    vmem, smem = pltpu.VMEM, pltpu.SMEM
    return pl.pallas_call(
        functools.partial(band_kernel, layouts, sharers),
        out_shape=jax.ShapeDtypeStruct((share, cols), jnp.float32),
        in_specs=[
            pl.BlockSpec(memory_space=vmem),
            pl.BlockSpec(memory_space=vmem),
            pl.BlockSpec(memory_space=smem),
            pl.BlockSpec(memory_space=vmem),
            pl.BlockSpec(memory_space=smem),
        ],
        out_specs=pl.BlockSpec(memory_space=vmem),
        scratch_shapes=[
            vmem((sharers, own_channels * tap_rows + 8, 128), jnp.float32),
            vmem((halo_rows + 2 * margin, cols), jnp.bfloat16),
            vmem((2, halo_rows + 2 * margin, cols), jnp.bfloat16),
            vmem((share + 2 * halo_rows, lanes), jnp.float32),
            vmem((near_rows, cols), jnp.float32),
            vmem((near_rows, cols), jnp.float32),
            vmem((edge, near_rows - step_rows + forward_window, cols), jnp.float32),
            vmem((channels, near_rows, cols), jnp.bfloat16),
            vmem((channels * step_rows, forward_depth), jnp.bfloat16),
            vmem((edge * step_rows, channels * adjoint_window), jnp.bfloat16),
            pltpu.SemaphoreType.DMA((sharers,)),
            pltpu.SemaphoreType.DMA((sharers,)),
            pltpu.SemaphoreType.DMA,
            pltpu.SemaphoreType.DMA((2,)),
        ],
        compiler_params=pltpu.CompilerParams(
            collective_id=0, has_side_effects=True, vmem_limit_bytes=48 * 1024 * 1024
        ),
    )(theta, target, occupancy, kernels, kernel_weights)


def solution(mesh):
    placed = (
        P(("group", "layout"), None),
        P(("group", "layout"), None),
        P(("group", "layout"), None),
        P(None, "kernel", None, None),
        P("kernel"),
    )
    return jax.shard_map(
        on_device,
        mesh=mesh,
        in_specs=placed,
        out_specs=P(("group", "layout", "kernel"), None),
        check_vma=False,
    )
```

```python
import functools
import jax
import jax.numpy as jnp
from jax import lax
from jax.experimental import pallas as pl
from jax.experimental.pallas import tpu as pltpu
from jax.sharding import PartitionSpec as P

steepness = 8.0
threshold = 1.0
step_rows = 16
margin = 16
halo_rows = 32
tap_rows = 24
tap_lanes = 32
mesh_id = pl.DeviceIdType.MESH


def band_kernel(
    layouts, sharers, theta_hbm, target_hbm, occupancy_hbm, kernels_hbm, weights_hbm, out_ref,
    theta_ref, target_ref, occupancy_ref, kernels_ref, weights_ref, load_sem, gathered, halo_out, halo_in, mask_ref, target_near, live_near, shifted, products, forward_ref,
    adjoint_ref, send_sem, recv_sem, halo_send_sem, halo_recv_sem,
):
    local_rows, cols = theta_ref.shape
    parts, edge, own_kernels, _ = kernels_ref.shape
    own_channels = parts * own_kernels
    channels = own_channels * sharers
    radius = edge // 2
    share = local_rows // sharers
    lanes = mask_ref.shape[1]
    forward_window = (shifted.shape[1] - (share + 2 * margin)) + step_rows
    forward_depth = forward_ref.shape[1]
    adjoint_window = step_rows + 2 * margin
    adjoint_depth = adjoint_ref.shape[1]
    column = lax.axis_index("layout")
    sharer = lax.axis_index("kernel")
    is_first = sharer == 0
    is_last = sharer == sharers - 1
    has_low = jnp.logical_and(is_first, column > 0)
    has_high = jnp.logical_and(is_last, column < layouts - 1)
    sends_up = jnp.logical_and(is_first, column < layouts - 1)
    sends_down = jnp.logical_and(is_last, column > 0)
    at_edge = jnp.logical_or(is_first, is_last)

    loads = [
        pltpu.make_async_copy(source, place, load_sem.at[index])
        for index, (source, place) in enumerate((
            (kernels_hbm, kernels_ref), (weights_hbm, weights_ref),
            (occupancy_hbm, occupancy_ref), (theta_hbm, theta_ref), (target_hbm, target_ref),
        ))
    ]
    for load in loads:
        load.start()

    barrier = pltpu.get_barrier_semaphore()
    for offset in range(1, sharers):
        pl.semaphore_signal(
            barrier, inc=1, device_id={"kernel": lax.rem(sharer + offset, sharers)},
            device_id_type=mesh_id,
        )

    @pl.when(jnp.logical_and(at_edge, column > 0))
    def _():
        pl.semaphore_signal(
            barrier, inc=1, device_id={"layout": column - 1}, device_id_type=mesh_id
        )

    @pl.when(jnp.logical_and(at_edge, column < layouts - 1))
    def _():
        pl.semaphore_signal(
            barrier, inc=1, device_id={"layout": column + 1}, device_id_type=mesh_id
        )

    gathered[0] = jnp.zeros(gathered.shape[1:], jnp.float32)
    loads[0].wait()
    loads[1].wait()
    for channel in range(own_channels):
        part, own = channel // own_kernels, channel % own_kernels
        lane_start = channel * tap_lanes
        taps = kernels_ref[part].astype(jnp.float32)
        for tap in range(edge):
            gathered[0, tap : tap + 1, lane_start : lane_start + edge] = taps[tap, own : own + 1]
        gathered[0, edge : edge + 1, lane_start : lane_start + edge] = jnp.broadcast_to(
            weights_ref[0:1, own : own + 1], (1, edge)
        )
    for load in loads[2:]:
        load.wait()

    tile_edge = cols // occupancy_ref.shape[1]
    lane = lax.broadcasted_iota(jnp.int32, (1, cols), 1)
    live_line = jnp.zeros((1, cols), jnp.float32)
    for tile in range(occupancy_ref.shape[1]):
        inside = jnp.logical_and(lane >= tile * tile_edge, lane < (tile + 1) * tile_edge)
        live_line = jnp.where(inside, occupancy_ref[0:1, tile : tile + 1].astype(jnp.float32), live_line)

    def mask_of(start, count):
        values = jax.nn.sigmoid(theta_ref[pl.ds(start, count), :].astype(jnp.float32)) * live_line
        return values.astype(jnp.bfloat16)

    def fill_halo(theta_start, target_start):
        halo_out[0:halo_rows, :] = mask_of(theta_start, halo_rows)
        halo_out[halo_rows : halo_rows + margin, :] = target_ref[pl.ds(target_start, margin), :]
        halo_out[halo_rows + margin :, :] = jnp.broadcast_to(live_line, (margin, cols)).astype(
            jnp.bfloat16
        )

    @pl.when(sends_up)
    def _():
        fill_halo(local_rows - halo_rows, local_rows - margin)

    @pl.when(sends_down)
    def _():
        fill_halo(0, 0)

    greeted = (column > 0).astype(jnp.int32) + (column < layouts - 1).astype(jnp.int32)
    pl.semaphore_wait(barrier, sharers - 1 + at_edge.astype(jnp.int32) * greeted)

    def halo_copy(side, neighbour):
        return pltpu.make_async_remote_copy(
            src_ref=halo_out, dst_ref=halo_in.at[side], send_sem=halo_send_sem,
            recv_sem=halo_recv_sem.at[side], device_id={"layout": neighbour},
            device_id_type=mesh_id,
        )

    @pl.when(sends_up)
    def _():
        halo_copy(0, column + 1).start()

    @pl.when(sends_down)
    def _():
        halo_copy(1, column - 1).start()

    tap_copies = [
        pltpu.make_async_remote_copy(
            src_ref=gathered.at[0], dst_ref=gathered.at[offset], send_sem=send_sem.at[offset],
            recv_sem=recv_sem.at[offset],
            device_id={"kernel": lax.rem(sharer + offset, sharers)}, device_id_type=mesh_id,
        )
        for offset in range(1, sharers)
    ]
    for copy in tap_copies:
        copy.start()

    first = pl.multiple_of(sharer * share, 32)
    mask_ref[:, cols:] = jnp.zeros((share + 2 * halo_rows, lanes - cols), jnp.float32)
    mask_ref[halo_rows : halo_rows + share, :cols] = mask_of(first, share).astype(jnp.float32)
    target_near[margin : margin + share, :] = target_ref[pl.ds(first, share), :].astype(
        jnp.float32
    )
    live_near[margin : margin + share, :] = jnp.broadcast_to(live_line, (share, cols))

    def place(mask_at, near_at, mask_values, target_values, live_values):
        mask_ref[mask_at : mask_at + halo_rows, :cols] = mask_values
        target_near[near_at : near_at + margin, :] = target_values
        live_near[near_at : near_at + margin, :] = live_values

    def place_own(mask_at, near_at, mask_start, near_start):
        place(
            mask_at, near_at, mask_of(mask_start, halo_rows).astype(jnp.float32),
            target_ref[pl.ds(near_start, margin), :].astype(jnp.float32),
            jnp.broadcast_to(live_line, (margin, cols)),
        )

    def place_received(mask_at, near_at, side):
        place(
            mask_at, near_at, halo_in[side, 0:halo_rows, :].astype(jnp.float32),
            halo_in[side, halo_rows : halo_rows + margin, :].astype(jnp.float32),
            halo_in[side, halo_rows + margin :, :].astype(jnp.float32),
        )

    def place_nothing(mask_at, near_at):
        place(
            mask_at, near_at, jnp.zeros((halo_rows, cols), jnp.float32),
            jnp.zeros((margin, cols), jnp.float32), jnp.zeros((margin, cols), jnp.float32),
        )

    high_mask, high_near = halo_rows + share, margin + share

    @pl.when(jnp.logical_not(is_first))
    def _():
        place_own(
            0, 0, pl.multiple_of(first - halo_rows, 32), pl.multiple_of(first - margin, 16)
        )

    @pl.when(jnp.logical_not(is_last))
    def _():
        after = pl.multiple_of(first + share, 32)
        place_own(high_mask, high_near, after, after)

    @pl.when(jnp.logical_and(is_first, column == 0))
    def _():
        place_nothing(0, 0)

    @pl.when(jnp.logical_and(is_last, column == layouts - 1))
    def _():
        place_nothing(high_mask, high_near)

    spread_row = lax.broadcasted_iota(jnp.int32, (128, forward_depth), 0)
    spread_lane = lax.broadcasted_iota(jnp.int32, (128, forward_depth), 1)
    spreads = []
    for channel in range(own_channels):
        ahead = spread_lane - forward_window * (spread_row - channel * tap_lanes)
        spread = jnp.logical_and(ahead >= 0, ahead < forward_window)
        spreads.append(jnp.where(spread, 1.0, 0.0).astype(jnp.bfloat16))
    line = lax.broadcasted_iota(jnp.int32, (tap_rows, forward_depth), 1)
    down = lax.broadcasted_iota(jnp.int32, (tap_rows, forward_depth), 0)
    chosen = jnp.zeros((tap_rows, forward_depth), jnp.float32)
    for tap in range(edge):
        chosen = jnp.where(line - forward_window * tap == down, 1.0, chosen)
    chosen = jnp.where(down < edge, chosen, 0.0)
    group_depth = sharers * adjoint_window
    turn_lanes = -(-group_depth // 128) * 128
    extent = (sharers, tap_rows, turn_lanes)
    slot_at = lax.broadcasted_iota(jnp.int32, extent, 0)
    row_at = lax.broadcasted_iota(jnp.int32, extent, 1)
    lane_at = lax.broadcasted_iota(jnp.int32, extent, 2)
    turn = lane_at == slot_at * adjoint_window + (margin + radius) - row_at
    turn = jnp.logical_and(turn, row_at < edge)
    turn = jnp.where(turn, 1.0, 0.0).reshape(sharers * tap_rows, turn_lanes).astype(jnp.bfloat16)

    @pl.when(has_low)
    def _():
        halo_copy(0, column - 1).wait_recv()
        place_received(0, 0, 0)

    @pl.when(has_high)
    def _():
        halo_copy(1, column + 1).wait_recv()
        place_received(high_mask, high_near, 1)

    skip = halo_rows - margin - radius
    around = mask_ref[skip : skip + shifted.shape[1], :]
    for tap in range(edge):
        moved = around if tap == radius else pltpu.roll(around, (radius - tap) % lanes, 1)
        shifted[tap] = moved[:, :cols]

    for copy in tap_copies:
        copy.wait()

    taps = gathered[...].reshape(sharers * tap_rows, 128).astype(jnp.bfloat16)
    lines = []
    for spread in spreads:
        wide = jnp.dot(taps, spread, preferred_element_type=jnp.float32)
        wide = wide.reshape(sharers, tap_rows, forward_depth)
        lines.append(jnp.sum(wide * chosen[None], axis=1))
    forward_line = jnp.concatenate(lines, axis=0)

    def toeplitz(lines):
        count, depth = lines.shape
        rows = jnp.broadcast_to(lines[:, None, :], (count, step_rows, depth))
        rows = rows.reshape(count * step_rows, depth)
        place_in_step = lax.broadcasted_iota(jnp.int32, rows.shape, 0) & (step_rows - 1)
        bit = 1
        while bit < step_rows:
            rows = jnp.where((place_in_step & bit) != 0, pltpu.roll(rows, bit, 1), rows)
            bit *= 2
        return rows.astype(jnp.bfloat16)

    forward_ref[...] = toeplitz(forward_line)
    turned = lax.dot_general(
        taps, turn, (((0,), (0,)), ((), ())), preferred_element_type=jnp.float32
    )
    rest = jnp.zeros((tap_rows, adjoint_depth - turn_lanes), jnp.float32)
    adjoint_line = None
    for channel in range(own_channels):
        piece = turned[channel * tap_lanes : channel * tap_lanes + tap_rows]
        piece = jnp.concatenate([piece, rest], axis=1)
        if channel:
            piece = pltpu.roll(piece, channel * group_depth, 1)
        adjoint_line = piece if adjoint_line is None else adjoint_line + piece
    adjoint_ref[...] = toeplitz(adjoint_line[:edge])

    def weight_of(channel):
        own, slot = channel // sharers, channel % sharers
        lane_start = own * tap_lanes
        return jnp.broadcast_to(
            gathered[slot, edge : edge + 1, lane_start : lane_start + 1], (step_rows, cols)
        )

    pad_depth = forward_depth - edge * forward_window

    def forward_step(index):
        start = index * step_rows
        windows = shifted[:, pl.ds(start, forward_window), :].reshape(-1, cols)
        windows = jnp.concatenate([windows, jnp.zeros((pad_depth, cols), jnp.float32)], axis=0)
        fields = jnp.dot(
            forward_ref[...], windows.astype(jnp.bfloat16), preferred_element_type=jnp.float32
        ).reshape(channels, step_rows, cols)
        intensity = jnp.zeros((step_rows, cols), jnp.float32)
        for channel in range(channels):
            intensity += weight_of(channel) * (fields[channel] * fields[channel])
        resist = jax.nn.sigmoid(steepness * (intensity - threshold))
        response = 2.0 * steepness * (resist - target_near[pl.ds(start, step_rows), :])
        response = response * resist * (1.0 - resist) * live_near[pl.ds(start, step_rows), :]
        for channel in range(channels):
            factor = 2.0 * weight_of(channel) * response
            products[channel, pl.ds(start, step_rows), :] = (factor * fields[channel]).astype(
                jnp.bfloat16
            )

    def adjoint_step(index):
        start = index * step_rows
        windows = products[:, pl.ds(start, adjoint_window), :].reshape(-1, cols)
        terms = jnp.dot(adjoint_ref[...], windows, preferred_element_type=jnp.float32)
        beside = jnp.zeros((step_rows, lanes - cols), jnp.float32)
        total = terms[radius * step_rows : (radius + 1) * step_rows, :]
        for tap in range(edge):
            if tap != radius:
                term = terms[tap * step_rows : (tap + 1) * step_rows, :]
                term = jnp.concatenate([term, beside], axis=1)
                total = total + pltpu.roll(term, (tap - radius) % lanes, 1)[:, :cols]
        out_ref[pl.ds(start, step_rows), :] = total * live_line

    for index in range((share + 2 * margin) // step_rows):
        forward_step(index)
    for index in range(share // step_rows):
        adjoint_step(index)

    @pl.when(sends_up)
    def _():
        halo_copy(0, column + 1).wait_send()

    @pl.when(sends_down)
    def _():
        halo_copy(1, column - 1).wait_send()


def on_device(theta, target, occupancy, kernels, kernel_weights):
    local_rows, cols = theta.shape
    layouts, sharers = lax.axis_size("layout"), lax.axis_size("kernel")
    own_channels = kernels.shape[0] * kernels.shape[1]
    channels = own_channels * sharers
    edge = kernels.shape[-1]
    share = local_rows // sharers
    lanes = cols + 128
    forward_window = -(-(step_rows + edge - 1) // 8) * 8
    forward_depth = -(-edge * forward_window // 128) * 128
    adjoint_window = step_rows + 2 * margin
    near_rows = share + 2 * margin
    vmem = pltpu.VMEM
    kernels = jnp.transpose(kernels, (0, 2, 1, 3))
    weights = kernel_weights.reshape(1, -1)
    return pl.pallas_call(
        functools.partial(band_kernel, layouts, sharers),
        out_shape=jax.ShapeDtypeStruct((share, cols), jnp.float32),
        in_specs=[pl.BlockSpec(memory_space=pltpu.HBM)] * 5,
        out_specs=pl.BlockSpec(memory_space=vmem),
        scratch_shapes=[
            vmem(theta.shape, theta.dtype),
            vmem(target.shape, target.dtype),
            vmem(occupancy.shape, occupancy.dtype),
            vmem(kernels.shape, kernels.dtype),
            vmem(weights.shape, weights.dtype),
            pltpu.SemaphoreType.DMA((5,)),
            vmem((sharers, tap_rows, 128), jnp.float32),
            vmem((halo_rows + 2 * margin, cols), jnp.bfloat16),
            vmem((2, halo_rows + 2 * margin, cols), jnp.bfloat16),
            vmem((share + 2 * halo_rows, lanes), jnp.float32),
            vmem((near_rows, cols), jnp.float32),
            vmem((near_rows, cols), jnp.float32),
            vmem((edge, near_rows - step_rows + forward_window, cols), jnp.float32),
            vmem((channels, near_rows, cols), jnp.bfloat16),
            vmem((channels * step_rows, forward_depth), jnp.bfloat16),
            vmem((edge * step_rows, channels * adjoint_window), jnp.bfloat16),
            pltpu.SemaphoreType.DMA((sharers,)),
            pltpu.SemaphoreType.DMA((sharers,)),
            pltpu.SemaphoreType.DMA,
            pltpu.SemaphoreType.DMA((2,)),
        ],
        compiler_params=pltpu.CompilerParams(
            collective_id=0, has_side_effects=True, vmem_limit_bytes=64 * 1024 * 1024 - 192 * 1024
        ),
    )(theta, target, occupancy, kernels, weights)


def solution(mesh):
    placed = (
        P(("group", "layout"), None),
        P(("group", "layout"), None),
        P(("group", "layout"), None),
        P(None, "kernel", None, None),
        P("kernel"),
    )
    return jax.shard_map(
        on_device,
        mesh=mesh,
        in_specs=placed,
        out_specs=P(("group", "layout", "kernel"), None),
        check_vma=False,
    )
```

```python
import functools
import jax
import jax.numpy as jnp
from jax import lax
from jax.experimental import pallas as pl
from jax.experimental.pallas import tpu as pltpu
from jax.sharding import PartitionSpec as P

steepness = 8.0
threshold = 1.0
step_rows = 16
margin = 16
halo_rows = 32
tap_rows = 24
tap_lanes = 32
mesh_id = pl.DeviceIdType.MESH


def band_kernel(
    layouts, sharers, theta_hbm, target_hbm, occupancy_hbm, kernels_hbm, weights_hbm, out_ref,
    theta_ref, target_ref, occupancy_ref, kernels_ref, weights_ref, load_sem, gathered, halo_out, halo_in, mask_ref, target_near, live_near, shifted, products, forward_ref,
    adjoint_ref, send_sem, recv_sem, halo_send_sem, halo_recv_sem,
):
    local_rows, cols = theta_ref.shape
    parts, edge, own_kernels, _ = kernels_ref.shape
    own_channels = parts * own_kernels
    channels = own_channels * sharers
    radius = edge // 2
    share = local_rows // sharers
    lanes = mask_ref.shape[1]
    forward_window = (shifted.shape[1] - (share + 2 * margin)) + step_rows
    forward_depth = forward_ref.shape[1]
    adjoint_window = step_rows + 2 * margin
    adjoint_depth = adjoint_ref.shape[1]
    column = lax.axis_index("layout")
    sharer = lax.axis_index("kernel")
    is_first = sharer == 0
    is_last = sharer == sharers - 1
    has_low = jnp.logical_and(is_first, column > 0)
    has_high = jnp.logical_and(is_last, column < layouts - 1)
    sends_up = jnp.logical_and(is_first, column < layouts - 1)
    sends_down = jnp.logical_and(is_last, column > 0)
    at_edge = jnp.logical_or(is_first, is_last)

    loads = [
        pltpu.make_async_copy(source, place, load_sem.at[index])
        for index, (source, place) in enumerate((
            (kernels_hbm, kernels_ref), (weights_hbm, weights_ref),
            (occupancy_hbm, occupancy_ref), (theta_hbm, theta_ref), (target_hbm, target_ref),
        ))
    ]
    for load in loads:
        load.start()

    barrier = pltpu.get_barrier_semaphore()
    for offset in range(1, sharers):
        pl.semaphore_signal(
            barrier, inc=1, device_id={"kernel": lax.rem(sharer + offset, sharers)},
            device_id_type=mesh_id,
        )

    @pl.when(jnp.logical_and(at_edge, column > 0))
    def _():
        pl.semaphore_signal(
            barrier, inc=1, device_id={"layout": column - 1}, device_id_type=mesh_id
        )

    @pl.when(jnp.logical_and(at_edge, column < layouts - 1))
    def _():
        pl.semaphore_signal(
            barrier, inc=1, device_id={"layout": column + 1}, device_id_type=mesh_id
        )

    gathered[0] = jnp.zeros(gathered.shape[1:], jnp.float32)
    loads[0].wait()
    loads[1].wait()
    for channel in range(own_channels):
        part, own = channel // own_kernels, channel % own_kernels
        lane_start = channel * tap_lanes
        taps = kernels_ref[part].astype(jnp.float32)
        for tap in range(edge):
            gathered[0, tap : tap + 1, lane_start : lane_start + edge] = taps[tap, own : own + 1]
        gathered[0, edge : edge + 1, lane_start : lane_start + edge] = jnp.broadcast_to(
            weights_ref[0:1, own : own + 1], (1, edge)
        )
    for load in loads[2:]:
        load.wait()

    tile_edge = cols // occupancy_ref.shape[1]
    lane = lax.broadcasted_iota(jnp.int32, (1, cols), 1)
    live_line = jnp.zeros((1, cols), jnp.float32)
    for tile in range(occupancy_ref.shape[1]):
        inside = jnp.logical_and(lane >= tile * tile_edge, lane < (tile + 1) * tile_edge)
        live_line = jnp.where(inside, occupancy_ref[0:1, tile : tile + 1].astype(jnp.float32), live_line)

    def mask_of(start, count):
        values = jax.nn.sigmoid(theta_ref[pl.ds(start, count), :].astype(jnp.float32)) * live_line
        return values.astype(jnp.bfloat16)

    def fill_halo(theta_start, target_start):
        halo_out[0:halo_rows, :] = mask_of(theta_start, halo_rows)
        halo_out[halo_rows : halo_rows + margin, :] = target_ref[pl.ds(target_start, margin), :]
        halo_out[halo_rows + margin :, :] = jnp.broadcast_to(live_line, (margin, cols)).astype(
            jnp.bfloat16
        )

    @pl.when(sends_up)
    def _():
        fill_halo(local_rows - halo_rows, local_rows - margin)

    @pl.when(sends_down)
    def _():
        fill_halo(0, 0)

    greeted = (column > 0).astype(jnp.int32) + (column < layouts - 1).astype(jnp.int32)
    pl.semaphore_wait(barrier, sharers - 1 + at_edge.astype(jnp.int32) * greeted)

    def halo_copy(side, neighbour):
        return pltpu.make_async_remote_copy(
            src_ref=halo_out, dst_ref=halo_in.at[side], send_sem=halo_send_sem,
            recv_sem=halo_recv_sem.at[side], device_id={"layout": neighbour},
            device_id_type=mesh_id,
        )

    @pl.when(sends_up)
    def _():
        halo_copy(0, column + 1).start()

    @pl.when(sends_down)
    def _():
        halo_copy(1, column - 1).start()

    tap_copies = [
        pltpu.make_async_remote_copy(
            src_ref=gathered.at[0], dst_ref=gathered.at[offset], send_sem=send_sem.at[offset],
            recv_sem=recv_sem.at[offset],
            device_id={"kernel": lax.rem(sharer + offset, sharers)}, device_id_type=mesh_id,
        )
        for offset in range(1, sharers)
    ]
    for copy in tap_copies:
        copy.start()

    first = pl.multiple_of(sharer * share, 32)
    mask_ref[:, cols:] = jnp.zeros((share + 2 * halo_rows, lanes - cols), jnp.float32)
    mask_ref[halo_rows : halo_rows + share, :cols] = mask_of(first, share).astype(jnp.float32)
    target_near[margin : margin + share, :] = target_ref[pl.ds(first, share), :].astype(
        jnp.float32
    )
    live_near[margin : margin + share, :] = jnp.broadcast_to(live_line, (share, cols))

    def place(mask_at, near_at, mask_values, target_values, live_values):
        mask_ref[mask_at : mask_at + halo_rows, :cols] = mask_values
        target_near[near_at : near_at + margin, :] = target_values
        live_near[near_at : near_at + margin, :] = live_values

    def place_own(mask_at, near_at, mask_start, near_start):
        place(
            mask_at, near_at, mask_of(mask_start, halo_rows).astype(jnp.float32),
            target_ref[pl.ds(near_start, margin), :].astype(jnp.float32),
            jnp.broadcast_to(live_line, (margin, cols)),
        )

    def place_received(mask_at, near_at, side):
        place(
            mask_at, near_at, halo_in[side, 0:halo_rows, :].astype(jnp.float32),
            halo_in[side, halo_rows : halo_rows + margin, :].astype(jnp.float32),
            halo_in[side, halo_rows + margin :, :].astype(jnp.float32),
        )

    def place_nothing(mask_at, near_at):
        place(
            mask_at, near_at, jnp.zeros((halo_rows, cols), jnp.float32),
            jnp.zeros((margin, cols), jnp.float32), jnp.zeros((margin, cols), jnp.float32),
        )

    high_mask, high_near = halo_rows + share, margin + share

    @pl.when(jnp.logical_not(is_first))
    def _():
        place_own(
            0, 0, pl.multiple_of(first - halo_rows, 32), pl.multiple_of(first - margin, 16)
        )

    @pl.when(jnp.logical_not(is_last))
    def _():
        after = pl.multiple_of(first + share, 32)
        place_own(high_mask, high_near, after, after)

    @pl.when(jnp.logical_and(is_first, column == 0))
    def _():
        place_nothing(0, 0)

    @pl.when(jnp.logical_and(is_last, column == layouts - 1))
    def _():
        place_nothing(high_mask, high_near)

    spread_row = lax.broadcasted_iota(jnp.int32, (128, forward_depth), 0)
    spread_lane = lax.broadcasted_iota(jnp.int32, (128, forward_depth), 1)
    spreads = []
    for channel in range(own_channels):
        ahead = spread_lane - forward_window * (spread_row - channel * tap_lanes)
        spread = jnp.logical_and(ahead >= 0, ahead < forward_window)
        spreads.append(jnp.where(spread, 1.0, 0.0).astype(jnp.bfloat16))
    line = lax.broadcasted_iota(jnp.int32, (tap_rows, forward_depth), 1)
    down = lax.broadcasted_iota(jnp.int32, (tap_rows, forward_depth), 0)
    chosen = jnp.zeros((tap_rows, forward_depth), jnp.float32)
    for tap in range(edge):
        chosen = jnp.where(line - forward_window * tap == down, 1.0, chosen)
    chosen = jnp.where(down < edge, chosen, 0.0)
    group_depth = sharers * adjoint_window
    turn_lanes = -(-group_depth // 128) * 128
    extent = (sharers, tap_rows, turn_lanes)
    slot_at = lax.broadcasted_iota(jnp.int32, extent, 0)
    row_at = lax.broadcasted_iota(jnp.int32, extent, 1)
    lane_at = lax.broadcasted_iota(jnp.int32, extent, 2)
    turn = lane_at == slot_at * adjoint_window + (margin + radius) - row_at
    turn = jnp.logical_and(turn, row_at < edge)
    turn = jnp.where(turn, 1.0, 0.0).reshape(sharers * tap_rows, turn_lanes).astype(jnp.bfloat16)

    @pl.when(has_low)
    def _():
        halo_copy(0, column - 1).wait_recv()
        place_received(0, 0, 0)

    @pl.when(has_high)
    def _():
        halo_copy(1, column + 1).wait_recv()
        place_received(high_mask, high_near, 1)

    skip = halo_rows - margin - radius
    around = mask_ref[skip : skip + shifted.shape[1], :]
    for tap in range(edge):
        moved = around if tap == radius else pltpu.roll(around, (radius - tap) % lanes, 1)
        shifted[tap] = moved[:, :cols]

    for copy in tap_copies:
        copy.wait()

    taps = gathered[...].reshape(sharers * tap_rows, 128).astype(jnp.bfloat16)
    lines = []
    for spread in spreads:
        wide = jnp.dot(taps, spread, preferred_element_type=jnp.float32)
        wide = wide.reshape(sharers, tap_rows, forward_depth)
        lines.append(jnp.sum(wide * chosen[None], axis=1))
    forward_line = jnp.concatenate(lines, axis=0)

    def toeplitz(lines):
        count, depth = lines.shape
        rows = jnp.broadcast_to(lines[:, None, :], (count, step_rows, depth))
        rows = rows.reshape(count * step_rows, depth)
        place_in_step = lax.broadcasted_iota(jnp.int32, rows.shape, 0) & (step_rows - 1)
        bit = 1
        while bit < step_rows:
            rows = jnp.where((place_in_step & bit) != 0, pltpu.roll(rows, bit, 1), rows)
            bit *= 2
        return rows.astype(jnp.bfloat16)

    forward_ref[...] = toeplitz(forward_line)
    turned = lax.dot_general(
        taps, turn, (((0,), (0,)), ((), ())), preferred_element_type=jnp.float32
    )
    rest = jnp.zeros((tap_rows, adjoint_depth - turn_lanes), jnp.float32)
    adjoint_line = None
    for channel in range(own_channels):
        piece = turned[channel * tap_lanes : channel * tap_lanes + tap_rows]
        piece = jnp.concatenate([piece, rest], axis=1)
        if channel:
            piece = pltpu.roll(piece, channel * group_depth, 1)
        adjoint_line = piece if adjoint_line is None else adjoint_line + piece
    adjoint_ref[...] = toeplitz(adjoint_line[:edge])

    def weight_of(channel):
        own, slot = channel // sharers, channel % sharers
        lane_start = own * tap_lanes
        return jnp.broadcast_to(
            gathered[slot, edge : edge + 1, lane_start : lane_start + 1], (step_rows, cols)
        )

    pad_depth = forward_depth - edge * forward_window

    def forward_step(index):
        start = index * step_rows
        windows = shifted[:, pl.ds(start, forward_window), :].reshape(-1, cols)
        windows = jnp.concatenate([windows, jnp.zeros((pad_depth, cols), jnp.float32)], axis=0)
        fields = jnp.dot(
            forward_ref[...], windows.astype(jnp.bfloat16), preferred_element_type=jnp.float32
        ).reshape(channels, step_rows, cols)
        intensity = jnp.zeros((step_rows, cols), jnp.float32)
        for channel in range(channels):
            intensity += weight_of(channel) * (fields[channel] * fields[channel])
        resist = jax.nn.sigmoid(steepness * (intensity - threshold))
        response = 2.0 * steepness * (resist - target_near[pl.ds(start, step_rows), :])
        response = response * resist * (1.0 - resist) * live_near[pl.ds(start, step_rows), :]
        for channel in range(channels):
            factor = 2.0 * weight_of(channel) * response
            products[channel, pl.ds(start, step_rows), :] = (factor * fields[channel]).astype(
                jnp.bfloat16
            )

    def adjoint_step(index):
        start = index * step_rows
        windows = products[:, pl.ds(start, adjoint_window), :].reshape(-1, cols)
        terms = jnp.dot(adjoint_ref[...], windows, preferred_element_type=jnp.float32)
        beside = jnp.zeros((step_rows, lanes - cols), jnp.float32)
        total = terms[radius * step_rows : (radius + 1) * step_rows, :]
        for tap in range(edge):
            if tap != radius:
                term = terms[tap * step_rows : (tap + 1) * step_rows, :]
                term = jnp.concatenate([term, beside], axis=1)
                total = total + pltpu.roll(term, (tap - radius) % lanes, 1)[:, :cols]
        out_ref[pl.ds(start, step_rows), :] = total * live_line

    for index in range((share + 2 * margin) // step_rows):
        forward_step(index)
    for index in range(share // step_rows):
        adjoint_step(index)

    @pl.when(sends_up)
    def _():
        halo_copy(0, column + 1).wait_send()

    @pl.when(sends_down)
    def _():
        halo_copy(1, column - 1).wait_send()


def on_device(theta, target, occupancy, kernels, kernel_weights):
    local_rows, cols = theta.shape
    layouts, sharers = lax.axis_size("layout"), lax.axis_size("kernel")
    own_channels = kernels.shape[0] * kernels.shape[1]
    channels = own_channels * sharers
    edge = kernels.shape[-1]
    share = local_rows // sharers
    lanes = cols + 128
    forward_window = -(-(step_rows + edge - 1) // 8) * 8
    forward_depth = -(-edge * forward_window // 128) * 128
    adjoint_window = step_rows + 2 * margin
    near_rows = share + 2 * margin
    vmem = pltpu.VMEM
    kernels = jnp.transpose(kernels, (0, 2, 1, 3))
    weights = kernel_weights.reshape(1, -1)
    return pl.pallas_call(
        functools.partial(band_kernel, layouts, sharers),
        out_shape=jax.ShapeDtypeStruct((share, cols), jnp.float32),
        in_specs=[pl.BlockSpec(memory_space=pltpu.HBM)] * 5,
        out_specs=pl.BlockSpec(memory_space=vmem),
        scratch_shapes=[
            vmem(theta.shape, theta.dtype),
            vmem(target.shape, target.dtype),
            vmem(occupancy.shape, occupancy.dtype),
            vmem(kernels.shape, kernels.dtype),
            vmem(weights.shape, weights.dtype),
            pltpu.SemaphoreType.DMA((5,)),
            vmem((sharers, tap_rows, 128), jnp.float32),
            vmem((halo_rows + 2 * margin, cols), jnp.bfloat16),
            vmem((2, halo_rows + 2 * margin, cols), jnp.bfloat16),
            vmem((share + 2 * halo_rows, lanes), jnp.float32),
            vmem((near_rows, cols), jnp.float32),
            vmem((near_rows, cols), jnp.float32),
            vmem((edge, near_rows - step_rows + forward_window, cols), jnp.float32),
            vmem((channels, near_rows, cols), jnp.bfloat16),
            vmem((channels * step_rows, forward_depth), jnp.bfloat16),
            vmem((edge * step_rows, channels * adjoint_window), jnp.bfloat16),
            pltpu.SemaphoreType.DMA((sharers,)),
            pltpu.SemaphoreType.DMA((sharers,)),
            pltpu.SemaphoreType.DMA,
            pltpu.SemaphoreType.DMA((2,)),
        ],
        compiler_params=pltpu.CompilerParams(
            collective_id=0, has_side_effects=True, vmem_limit_bytes=48 * 1024 * 1024
        ),
    )(*(pltpu.with_memory_space_constraint(x, pltpu.HBM) for x in (theta, target, occupancy, kernels, weights)))


def solution(mesh):
    placed = (
        P(("group", "layout"), None),
        P(("group", "layout"), None),
        P(("group", "layout"), None),
        P(None, "kernel", None, None),
        P("kernel"),
    )
    return jax.shard_map(
        on_device,
        mesh=mesh,
        in_specs=placed,
        out_specs=P(("group", "layout", "kernel"), None),
        check_vma=False,
    )
```

```python
import functools
import jax
import jax.numpy as jnp
from jax import lax
from jax.experimental import pallas as pl
from jax.experimental.pallas import tpu as pltpu
from jax.sharding import PartitionSpec as P

steepness = 8.0
threshold = 1.0
step_rows = 16
margin = 16
halo_rows = 32
tap_rows = 24
tap_lanes = 32
mesh_id = pl.DeviceIdType.MESH


def band_kernel(
    layouts, sharers, theta_hbm, target_hbm, occupancy_hbm, kernels_hbm, weights_hbm, out_ref,
    theta_ref, target_ref, occupancy_ref, kernels_ref, weights_ref, load_sem, gathered, halo_out, halo_in, mask_ref, target_near, live_near, shifted, products, forward_ref,
    adjoint_ref, send_sem, recv_sem, halo_send_sem, halo_recv_sem,
):
    local_rows, cols = theta_ref.shape
    parts, edge, own_kernels, _ = kernels_ref.shape
    own_channels = parts * own_kernels
    channels = own_channels * sharers
    radius = edge // 2
    share = local_rows // sharers
    lanes = mask_ref.shape[1]
    forward_window = (shifted.shape[1] - (share + 2 * margin)) + step_rows
    forward_depth = forward_ref.shape[1]
    adjoint_window = step_rows + 2 * margin
    adjoint_depth = adjoint_ref.shape[1]
    column = lax.axis_index("layout")
    sharer = lax.axis_index("kernel")
    is_first = sharer == 0
    is_last = sharer == sharers - 1
    has_low = jnp.logical_and(is_first, column > 0)
    has_high = jnp.logical_and(is_last, column < layouts - 1)
    sends_up = jnp.logical_and(is_first, column < layouts - 1)
    sends_down = jnp.logical_and(is_last, column > 0)
    at_edge = jnp.logical_or(is_first, is_last)

    loads = [
        pltpu.make_async_copy(source, place, load_sem.at[index])
        for index, (source, place) in enumerate((
            (kernels_hbm, kernels_ref), (weights_hbm, weights_ref),
            (occupancy_hbm, occupancy_ref), (theta_hbm, theta_ref), (target_hbm, target_ref),
        ))
    ]
    for load in loads:
        load.start()

    barrier = pltpu.get_barrier_semaphore()
    for offset in range(1, sharers):
        pl.semaphore_signal(
            barrier, inc=1, device_id={"kernel": lax.rem(sharer + offset, sharers)},
            device_id_type=mesh_id,
        )

    @pl.when(jnp.logical_and(at_edge, column > 0))
    def _():
        pl.semaphore_signal(
            barrier, inc=1, device_id={"layout": column - 1}, device_id_type=mesh_id
        )

    @pl.when(jnp.logical_and(at_edge, column < layouts - 1))
    def _():
        pl.semaphore_signal(
            barrier, inc=1, device_id={"layout": column + 1}, device_id_type=mesh_id
        )

    gathered[0] = jnp.zeros(gathered.shape[1:], jnp.float32)
    loads[0].wait()
    loads[1].wait()
    for channel in range(own_channels):
        part, own = channel // own_kernels, channel % own_kernels
        lane_start = channel * tap_lanes
        taps = kernels_ref[part].astype(jnp.float32)
        for tap in range(edge):
            gathered[0, tap : tap + 1, lane_start : lane_start + edge] = taps[tap, own : own + 1]
        gathered[0, edge : edge + 1, lane_start : lane_start + edge] = jnp.broadcast_to(
            weights_ref[0:1, own : own + 1], (1, edge)
        )
    greeted = (column > 0).astype(jnp.int32) + (column < layouts - 1).astype(jnp.int32)
    pl.semaphore_wait(barrier, sharers - 1 + at_edge.astype(jnp.int32) * greeted)

    tap_copies = [
        pltpu.make_async_remote_copy(
            src_ref=gathered.at[0], dst_ref=gathered.at[offset], send_sem=send_sem.at[offset],
            recv_sem=recv_sem.at[offset],
            device_id={"kernel": lax.rem(sharer + offset, sharers)}, device_id_type=mesh_id,
        )
        for offset in range(1, sharers)
    ]
    for copy in tap_copies:
        copy.start()

    for load in loads[2:]:
        load.wait()

    tile_edge = cols // occupancy_ref.shape[1]
    lane = lax.broadcasted_iota(jnp.int32, (1, cols), 1)
    live_line = jnp.zeros((1, cols), jnp.float32)
    for tile in range(occupancy_ref.shape[1]):
        inside = jnp.logical_and(lane >= tile * tile_edge, lane < (tile + 1) * tile_edge)
        live_line = jnp.where(inside, occupancy_ref[0:1, tile : tile + 1].astype(jnp.float32), live_line)

    def mask_of(start, count):
        values = jax.nn.sigmoid(theta_ref[pl.ds(start, count), :].astype(jnp.float32)) * live_line
        return values.astype(jnp.bfloat16)

    def fill_halo(theta_start, target_start):
        halo_out[0:halo_rows, :] = mask_of(theta_start, halo_rows)
        halo_out[halo_rows : halo_rows + margin, :] = target_ref[pl.ds(target_start, margin), :]
        halo_out[halo_rows + margin :, :] = jnp.broadcast_to(live_line, (margin, cols)).astype(
            jnp.bfloat16
        )

    @pl.when(sends_up)
    def _():
        fill_halo(local_rows - halo_rows, local_rows - margin)

    @pl.when(sends_down)
    def _():
        fill_halo(0, 0)

    def halo_copy(side, neighbour):
        return pltpu.make_async_remote_copy(
            src_ref=halo_out, dst_ref=halo_in.at[side], send_sem=halo_send_sem,
            recv_sem=halo_recv_sem.at[side], device_id={"layout": neighbour},
            device_id_type=mesh_id,
        )

    @pl.when(sends_up)
    def _():
        halo_copy(0, column + 1).start()

    @pl.when(sends_down)
    def _():
        halo_copy(1, column - 1).start()

    first = pl.multiple_of(sharer * share, 32)
    mask_ref[:, cols:] = jnp.zeros((share + 2 * halo_rows, lanes - cols), jnp.float32)
    mask_ref[halo_rows : halo_rows + share, :cols] = mask_of(first, share).astype(jnp.float32)
    target_near[margin : margin + share, :] = target_ref[pl.ds(first, share), :].astype(
        jnp.float32
    )
    live_near[margin : margin + share, :] = jnp.broadcast_to(live_line, (share, cols))

    def place(mask_at, near_at, mask_values, target_values, live_values):
        mask_ref[mask_at : mask_at + halo_rows, :cols] = mask_values
        target_near[near_at : near_at + margin, :] = target_values
        live_near[near_at : near_at + margin, :] = live_values

    def place_own(mask_at, near_at, mask_start, near_start):
        place(
            mask_at, near_at, mask_of(mask_start, halo_rows).astype(jnp.float32),
            target_ref[pl.ds(near_start, margin), :].astype(jnp.float32),
            jnp.broadcast_to(live_line, (margin, cols)),
        )

    def place_received(mask_at, near_at, side):
        place(
            mask_at, near_at, halo_in[side, 0:halo_rows, :].astype(jnp.float32),
            halo_in[side, halo_rows : halo_rows + margin, :].astype(jnp.float32),
            halo_in[side, halo_rows + margin :, :].astype(jnp.float32),
        )

    def place_nothing(mask_at, near_at):
        place(
            mask_at, near_at, jnp.zeros((halo_rows, cols), jnp.float32),
            jnp.zeros((margin, cols), jnp.float32), jnp.zeros((margin, cols), jnp.float32),
        )

    high_mask, high_near = halo_rows + share, margin + share

    @pl.when(jnp.logical_not(is_first))
    def _():
        place_own(
            0, 0, pl.multiple_of(first - halo_rows, 32), pl.multiple_of(first - margin, 16)
        )

    @pl.when(jnp.logical_not(is_last))
    def _():
        after = pl.multiple_of(first + share, 32)
        place_own(high_mask, high_near, after, after)

    @pl.when(jnp.logical_and(is_first, column == 0))
    def _():
        place_nothing(0, 0)

    @pl.when(jnp.logical_and(is_last, column == layouts - 1))
    def _():
        place_nothing(high_mask, high_near)

    spread_row = lax.broadcasted_iota(jnp.int32, (128, forward_depth), 0)
    spread_lane = lax.broadcasted_iota(jnp.int32, (128, forward_depth), 1)
    spreads = []
    for channel in range(own_channels):
        ahead = spread_lane - forward_window * (spread_row - channel * tap_lanes)
        spread = jnp.logical_and(ahead >= 0, ahead < forward_window)
        spreads.append(jnp.where(spread, 1.0, 0.0).astype(jnp.bfloat16))
    line = lax.broadcasted_iota(jnp.int32, (tap_rows, forward_depth), 1)
    down = lax.broadcasted_iota(jnp.int32, (tap_rows, forward_depth), 0)
    chosen = jnp.zeros((tap_rows, forward_depth), jnp.float32)
    for tap in range(edge):
        chosen = jnp.where(line - forward_window * tap == down, 1.0, chosen)
    chosen = jnp.where(down < edge, chosen, 0.0)
    group_depth = sharers * adjoint_window
    turn_lanes = -(-group_depth // 128) * 128
    extent = (sharers, tap_rows, turn_lanes)
    slot_at = lax.broadcasted_iota(jnp.int32, extent, 0)
    row_at = lax.broadcasted_iota(jnp.int32, extent, 1)
    lane_at = lax.broadcasted_iota(jnp.int32, extent, 2)
    turn = lane_at == slot_at * adjoint_window + (margin + radius) - row_at
    turn = jnp.logical_and(turn, row_at < edge)
    turn = jnp.where(turn, 1.0, 0.0).reshape(sharers * tap_rows, turn_lanes).astype(jnp.bfloat16)

    @pl.when(has_low)
    def _():
        halo_copy(0, column - 1).wait_recv()
        place_received(0, 0, 0)

    @pl.when(has_high)
    def _():
        halo_copy(1, column + 1).wait_recv()
        place_received(high_mask, high_near, 1)

    skip = halo_rows - margin - radius
    around = mask_ref[skip : skip + shifted.shape[1], :]
    for tap in range(edge):
        moved = around if tap == radius else pltpu.roll(around, (radius - tap) % lanes, 1)
        shifted[tap] = moved[:, :cols]

    for copy in tap_copies:
        copy.wait()

    taps = gathered[...].reshape(sharers * tap_rows, 128).astype(jnp.bfloat16)
    lines = []
    for spread in spreads:
        wide = jnp.dot(taps, spread, preferred_element_type=jnp.float32)
        wide = wide.reshape(sharers, tap_rows, forward_depth)
        lines.append(jnp.sum(wide * chosen[None], axis=1))
    forward_line = jnp.concatenate(lines, axis=0)

    def toeplitz(lines):
        count, depth = lines.shape
        rows = jnp.concatenate(
            [
                pltpu.roll(
                    jnp.broadcast_to(lines[row : row + 1], (step_rows, depth)), 0, 1, stride=1,
                    stride_axis=0,
                )
                for row in range(count)
            ],
            axis=0,
        )
        return rows.astype(jnp.bfloat16)

    forward_ref[...] = toeplitz(forward_line)
    turned = lax.dot_general(
        taps, turn, (((0,), (0,)), ((), ())), preferred_element_type=jnp.float32
    )
    rest = jnp.zeros((tap_rows, adjoint_depth - turn_lanes), jnp.float32)
    adjoint_line = None
    for channel in range(own_channels):
        piece = turned[channel * tap_lanes : channel * tap_lanes + tap_rows]
        piece = jnp.concatenate([piece, rest], axis=1)
        if channel:
            piece = pltpu.roll(piece, channel * group_depth, 1)
        adjoint_line = piece if adjoint_line is None else adjoint_line + piece
    adjoint_ref[...] = toeplitz(adjoint_line[:edge])

    def weight_of(channel):
        own, slot = channel // sharers, channel % sharers
        lane_start = own * tap_lanes
        return jnp.broadcast_to(
            gathered[slot, edge : edge + 1, lane_start : lane_start + 1], (step_rows, cols)
        )

    pad_depth = forward_depth - edge * forward_window

    def forward_step(index):
        start = index * step_rows
        windows = shifted[:, pl.ds(start, forward_window), :].reshape(-1, cols)
        windows = jnp.concatenate([windows, jnp.zeros((pad_depth, cols), jnp.float32)], axis=0)
        fields = jnp.dot(
            forward_ref[...], windows.astype(jnp.bfloat16), preferred_element_type=jnp.float32
        ).reshape(channels, step_rows, cols)
        intensity = jnp.zeros((step_rows, cols), jnp.float32)
        for channel in range(channels):
            intensity += weight_of(channel) * (fields[channel] * fields[channel])
        resist = jax.nn.sigmoid(steepness * (intensity - threshold))
        response = 2.0 * steepness * (resist - target_near[pl.ds(start, step_rows), :])
        response = response * resist * (1.0 - resist) * live_near[pl.ds(start, step_rows), :]
        for channel in range(channels):
            factor = 2.0 * weight_of(channel) * response
            products[channel, pl.ds(start, step_rows), :] = (factor * fields[channel]).astype(
                jnp.bfloat16
            )

    def adjoint_step(index):
        start = index * step_rows
        windows = products[:, pl.ds(start, adjoint_window), :].reshape(-1, cols)
        terms = jnp.dot(adjoint_ref[...], windows, preferred_element_type=jnp.float32)
        beside = jnp.zeros((step_rows, lanes - cols), jnp.float32)
        total = terms[radius * step_rows : (radius + 1) * step_rows, :]
        for tap in range(edge):
            if tap != radius:
                term = terms[tap * step_rows : (tap + 1) * step_rows, :]
                term = jnp.concatenate([term, beside], axis=1)
                total = total + pltpu.roll(term, (tap - radius) % lanes, 1)[:, :cols]
        out_ref[pl.ds(start, step_rows), :] = total * live_line

    for index in range((share + 2 * margin) // step_rows):
        forward_step(index)
    for index in range(share // step_rows):
        adjoint_step(index)

    @pl.when(sends_up)
    def _():
        halo_copy(0, column + 1).wait_send()

    @pl.when(sends_down)
    def _():
        halo_copy(1, column - 1).wait_send()


def on_device(theta, target, occupancy, kernels, kernel_weights):
    local_rows, cols = theta.shape
    layouts, sharers = lax.axis_size("layout"), lax.axis_size("kernel")
    own_channels = kernels.shape[0] * kernels.shape[1]
    channels = own_channels * sharers
    edge = kernels.shape[-1]
    share = local_rows // sharers
    lanes = cols + 128
    forward_window = -(-(step_rows + edge - 1) // 8) * 8
    forward_depth = -(-edge * forward_window // 128) * 128
    adjoint_window = step_rows + 2 * margin
    near_rows = share + 2 * margin
    vmem = pltpu.VMEM
    kernels = jnp.transpose(kernels, (0, 2, 1, 3))
    weights = kernel_weights.reshape(1, -1)
    return pl.pallas_call(
        functools.partial(band_kernel, layouts, sharers),
        out_shape=jax.ShapeDtypeStruct((share, cols), jnp.float32),
        in_specs=[pl.BlockSpec(memory_space=pltpu.HBM)] * 5,
        out_specs=pl.BlockSpec(memory_space=vmem),
        scratch_shapes=[
            vmem(theta.shape, theta.dtype),
            vmem(target.shape, target.dtype),
            vmem(occupancy.shape, occupancy.dtype),
            vmem(kernels.shape, kernels.dtype),
            vmem(weights.shape, weights.dtype),
            pltpu.SemaphoreType.DMA((5,)),
            vmem((sharers, tap_rows, 128), jnp.float32),
            vmem((halo_rows + 2 * margin, cols), jnp.bfloat16),
            vmem((2, halo_rows + 2 * margin, cols), jnp.bfloat16),
            vmem((share + 2 * halo_rows, lanes), jnp.float32),
            vmem((near_rows, cols), jnp.float32),
            vmem((near_rows, cols), jnp.float32),
            vmem((edge, near_rows - step_rows + forward_window, cols), jnp.float32),
            vmem((channels, near_rows, cols), jnp.bfloat16),
            vmem((channels * step_rows, forward_depth), jnp.bfloat16),
            vmem((edge * step_rows, channels * adjoint_window), jnp.bfloat16),
            pltpu.SemaphoreType.DMA((sharers,)),
            pltpu.SemaphoreType.DMA((sharers,)),
            pltpu.SemaphoreType.DMA,
            pltpu.SemaphoreType.DMA((2,)),
        ],
        compiler_params=pltpu.CompilerParams(
            collective_id=0, has_side_effects=True, vmem_limit_bytes=48 * 1024 * 1024
        ),
    )(*(pltpu.with_memory_space_constraint(x, pltpu.HBM) for x in (theta, target, occupancy, kernels, weights)))


def solution(mesh):
    placed = (
        P(("group", "layout"), None),
        P(("group", "layout"), None),
        P(("group", "layout"), None),
        P(None, "kernel", None, None),
        P("kernel"),
    )
    return jax.shard_map(
        on_device,
        mesh=mesh,
        in_specs=placed,
        out_specs=P(("group", "layout", "kernel"), None),
        check_vma=False,
    )
```

```python
import functools
import jax
import jax.numpy as jnp
from jax import lax
from jax.experimental import pallas as pl
from jax.experimental.pallas import tpu as pltpu
from jax.sharding import PartitionSpec as P

steepness = 8.0
threshold = 1.0
step_rows = 16
margin = 16
halo_rows = 32
tap_rows = 24
tap_lanes = 32
mesh_id = pl.DeviceIdType.MESH


def band_kernel(
    layouts, sharers, theta_hbm, target_hbm, occupancy_hbm, kernels_hbm, weights_hbm, out_ref,
    theta_ref, target_ref, occupancy_ref, kernels_ref, weights_ref, load_sem, gathered, halo_out, halo_in, mask_ref, target_near, live_near, shifted, products, forward_ref,
    adjoint_ref, send_sem, recv_sem, halo_send_sem, halo_recv_sem,
):
    local_rows, cols = theta_ref.shape
    parts, edge, own_kernels, _ = kernels_ref.shape
    own_channels = parts * own_kernels
    channels = own_channels * sharers
    radius = edge // 2
    share = local_rows // sharers
    lanes = mask_ref.shape[1]
    forward_window = (shifted.shape[1] - (share + 2 * margin)) + step_rows
    forward_depth = forward_ref.shape[1]
    adjoint_window = step_rows + 2 * margin
    adjoint_depth = adjoint_ref.shape[1]
    column = lax.axis_index("layout")
    sharer = lax.axis_index("kernel")
    is_first = sharer == 0
    is_last = sharer == sharers - 1
    has_low = jnp.logical_and(is_first, column > 0)
    has_high = jnp.logical_and(is_last, column < layouts - 1)
    sends_up = jnp.logical_and(is_first, column < layouts - 1)
    sends_down = jnp.logical_and(is_last, column > 0)
    at_edge = jnp.logical_or(is_first, is_last)

    loads = [
        pltpu.make_async_copy(source, place, load_sem.at[index])
        for index, (source, place) in enumerate((
            (kernels_hbm, kernels_ref), (weights_hbm, weights_ref),
            (occupancy_hbm, occupancy_ref), (theta_hbm, theta_ref), (target_hbm, target_ref),
        ))
    ]
    for load in loads:
        load.start()

    barrier = pltpu.get_barrier_semaphore()
    for offset in range(1, sharers):
        pl.semaphore_signal(
            barrier, inc=1, device_id={"kernel": lax.rem(sharer + offset, sharers)},
            device_id_type=mesh_id,
        )

    @pl.when(jnp.logical_and(at_edge, column > 0))
    def _():
        pl.semaphore_signal(
            barrier, inc=1, device_id={"layout": column - 1}, device_id_type=mesh_id
        )

    @pl.when(jnp.logical_and(at_edge, column < layouts - 1))
    def _():
        pl.semaphore_signal(
            barrier, inc=1, device_id={"layout": column + 1}, device_id_type=mesh_id
        )

    gathered[0] = jnp.zeros(gathered.shape[1:], jnp.float32)
    loads[0].wait()
    loads[1].wait()
    for channel in range(own_channels):
        part, own = channel // own_kernels, channel % own_kernels
        lane_start = channel * tap_lanes
        taps = kernels_ref[part].astype(jnp.float32)
        for tap in range(edge):
            gathered[0, tap : tap + 1, lane_start : lane_start + edge] = taps[tap, own : own + 1]
        gathered[0, edge : edge + 1, lane_start : lane_start + edge] = jnp.broadcast_to(
            weights_ref[0:1, own : own + 1], (1, edge)
        )
    greeted = (column > 0).astype(jnp.int32) + (column < layouts - 1).astype(jnp.int32)
    pl.semaphore_wait(barrier, sharers - 1 + at_edge.astype(jnp.int32) * greeted)

    tap_copies = [
        pltpu.make_async_remote_copy(
            src_ref=gathered.at[0], dst_ref=gathered.at[offset], send_sem=send_sem.at[offset],
            recv_sem=recv_sem.at[offset],
            device_id={"kernel": lax.rem(sharer + offset, sharers)}, device_id_type=mesh_id,
        )
        for offset in range(1, sharers)
    ]
    for copy in tap_copies:
        copy.start()

    for load in loads[2:]:
        load.wait()

    tile_edge = cols // occupancy_ref.shape[1]
    lane = lax.broadcasted_iota(jnp.int32, (1, cols), 1)
    live_line = jnp.zeros((1, cols), jnp.float32)
    for tile in range(occupancy_ref.shape[1]):
        inside = jnp.logical_and(lane >= tile * tile_edge, lane < (tile + 1) * tile_edge)
        live_line = jnp.where(inside, occupancy_ref[0:1, tile : tile + 1].astype(jnp.float32), live_line)

    def mask_of(start, count):
        values = jax.nn.sigmoid(theta_ref[pl.ds(start, count), :].astype(jnp.float32)) * live_line
        return values.astype(jnp.bfloat16)

    def fill_halo(theta_start, target_start):
        halo_out[0:halo_rows, :] = mask_of(theta_start, halo_rows)
        halo_out[halo_rows : halo_rows + margin, :] = target_ref[pl.ds(target_start, margin), :]
        halo_out[halo_rows + margin :, :] = jnp.broadcast_to(live_line, (margin, cols)).astype(
            jnp.bfloat16
        )

    @pl.when(sends_up)
    def _():
        fill_halo(local_rows - halo_rows, local_rows - margin)

    @pl.when(sends_down)
    def _():
        fill_halo(0, 0)

    def halo_copy(side, neighbour):
        return pltpu.make_async_remote_copy(
            src_ref=halo_out, dst_ref=halo_in.at[side], send_sem=halo_send_sem,
            recv_sem=halo_recv_sem.at[side], device_id={"layout": neighbour},
            device_id_type=mesh_id,
        )

    @pl.when(sends_up)
    def _():
        halo_copy(0, column + 1).start()

    @pl.when(sends_down)
    def _():
        halo_copy(1, column - 1).start()

    first = pl.multiple_of(sharer * share, 32)
    mask_ref[:, cols:] = jnp.zeros((share + 2 * halo_rows, lanes - cols), jnp.float32)
    mask_ref[halo_rows : halo_rows + share, :cols] = mask_of(first, share).astype(jnp.float32)
    target_near[margin : margin + share, :] = target_ref[pl.ds(first, share), :].astype(
        jnp.float32
    )
    live_near[margin : margin + share, :] = jnp.broadcast_to(live_line, (share, cols))

    def place(mask_at, near_at, mask_values, target_values, live_values):
        mask_ref[mask_at : mask_at + halo_rows, :cols] = mask_values
        target_near[near_at : near_at + margin, :] = target_values
        live_near[near_at : near_at + margin, :] = live_values

    def place_own(mask_at, near_at, mask_start, near_start):
        place(
            mask_at, near_at, mask_of(mask_start, halo_rows).astype(jnp.float32),
            target_ref[pl.ds(near_start, margin), :].astype(jnp.float32),
            jnp.broadcast_to(live_line, (margin, cols)),
        )

    def place_received(mask_at, near_at, side):
        place(
            mask_at, near_at, halo_in[side, 0:halo_rows, :].astype(jnp.float32),
            halo_in[side, halo_rows : halo_rows + margin, :].astype(jnp.float32),
            halo_in[side, halo_rows + margin :, :].astype(jnp.float32),
        )

    def place_nothing(mask_at, near_at):
        place(
            mask_at, near_at, jnp.zeros((halo_rows, cols), jnp.float32),
            jnp.zeros((margin, cols), jnp.float32), jnp.zeros((margin, cols), jnp.float32),
        )

    high_mask, high_near = halo_rows + share, margin + share

    @pl.when(jnp.logical_not(is_first))
    def _():
        place_own(
            0, 0, pl.multiple_of(first - halo_rows, 32), pl.multiple_of(first - margin, 16)
        )

    @pl.when(jnp.logical_not(is_last))
    def _():
        after = pl.multiple_of(first + share, 32)
        place_own(high_mask, high_near, after, after)

    @pl.when(jnp.logical_and(is_first, column == 0))
    def _():
        place_nothing(0, 0)

    @pl.when(jnp.logical_and(is_last, column == layouts - 1))
    def _():
        place_nothing(high_mask, high_near)

    spread_row = lax.broadcasted_iota(jnp.int32, (128, forward_depth), 0)
    spread_lane = lax.broadcasted_iota(jnp.int32, (128, forward_depth), 1)
    spreads = []
    for channel in range(own_channels):
        ahead = spread_lane - forward_window * (spread_row - channel * tap_lanes)
        spread = jnp.logical_and(ahead >= 0, ahead < forward_window)
        spreads.append(jnp.where(spread, 1.0, 0.0).astype(jnp.bfloat16))
    line = lax.broadcasted_iota(jnp.int32, (tap_rows, forward_depth), 1)
    down = lax.broadcasted_iota(jnp.int32, (tap_rows, forward_depth), 0)
    chosen = jnp.zeros((tap_rows, forward_depth), jnp.float32)
    for tap in range(edge):
        chosen = jnp.where(line - forward_window * tap == down, 1.0, chosen)
    chosen = jnp.where(down < edge, chosen, 0.0)
    group_depth = sharers * adjoint_window
    turn_lanes = -(-group_depth // 128) * 128
    extent = (sharers, tap_rows, turn_lanes)
    slot_at = lax.broadcasted_iota(jnp.int32, extent, 0)
    row_at = lax.broadcasted_iota(jnp.int32, extent, 1)
    lane_at = lax.broadcasted_iota(jnp.int32, extent, 2)
    turn = lane_at == slot_at * adjoint_window + (margin + radius) - row_at
    turn = jnp.logical_and(turn, row_at < edge)
    turn = jnp.where(turn, 1.0, 0.0).reshape(sharers * tap_rows, turn_lanes).astype(jnp.bfloat16)

    @pl.when(has_low)
    def _():
        halo_copy(0, column - 1).wait_recv()
        place_received(0, 0, 0)

    @pl.when(has_high)
    def _():
        halo_copy(1, column + 1).wait_recv()
        place_received(high_mask, high_near, 1)

    skip = halo_rows - margin - radius
    around = mask_ref[skip : skip + shifted.shape[1], :]
    for tap in range(edge):
        moved = around if tap == radius else pltpu.roll(around, (radius - tap) % lanes, 1)
        shifted[tap] = moved[:, :cols]

    for copy in tap_copies:
        copy.wait()

    taps = gathered[...].reshape(sharers * tap_rows, 128).astype(jnp.bfloat16)
    lines = []
    for spread in spreads:
        wide = jnp.dot(taps, spread, preferred_element_type=jnp.float32)
        wide = wide.reshape(sharers, tap_rows, forward_depth)
        lines.append(jnp.sum(wide * chosen[None], axis=1))
    forward_line = jnp.concatenate(lines, axis=0)

    def toeplitz(lines):
        count, depth = lines.shape
        rows = jnp.concatenate(
            [
                pltpu.roll(
                    jnp.broadcast_to(lines[row : row + 1], (step_rows, depth)), 0, 1, stride=1,
                    stride_axis=0,
                )
                for row in range(count)
            ],
            axis=0,
        )
        return rows.astype(jnp.bfloat16)

    forward_ref[...] = toeplitz(forward_line)

    def weight_of(channel):
        own, slot = channel // sharers, channel % sharers
        lane_start = own * tap_lanes
        return jnp.broadcast_to(
            gathered[slot, edge : edge + 1, lane_start : lane_start + 1], (step_rows, cols)
        )

    pad_depth = forward_depth - edge * forward_window

    def forward_step(index):
        start = index * step_rows
        windows = shifted[:, pl.ds(start, forward_window), :].reshape(-1, cols)
        windows = jnp.concatenate([windows, jnp.zeros((pad_depth, cols), jnp.float32)], axis=0)
        fields = jnp.dot(
            forward_ref[...], windows.astype(jnp.bfloat16), preferred_element_type=jnp.float32
        ).reshape(channels, step_rows, cols)
        intensity = jnp.zeros((step_rows, cols), jnp.float32)
        for channel in range(channels):
            intensity += weight_of(channel) * (fields[channel] * fields[channel])
        resist = jax.nn.sigmoid(steepness * (intensity - threshold))
        response = 2.0 * steepness * (resist - target_near[pl.ds(start, step_rows), :])
        response = response * resist * (1.0 - resist) * live_near[pl.ds(start, step_rows), :]
        for channel in range(channels):
            factor = 2.0 * weight_of(channel) * response
            products[channel, pl.ds(start, step_rows), :] = (factor * fields[channel]).astype(
                jnp.bfloat16
            )

    def build_adjoint():
        turned = lax.dot_general(
            taps, turn, (((0,), (0,)), ((), ())), preferred_element_type=jnp.float32
        )
        rest = jnp.zeros((tap_rows, adjoint_depth - turn_lanes), jnp.float32)
        adjoint_line = None
        for channel in range(own_channels):
            piece = turned[channel * tap_lanes : channel * tap_lanes + tap_rows]
            piece = jnp.concatenate([piece, rest], axis=1)
            if channel:
                piece = pltpu.roll(piece, channel * group_depth, 1)
            adjoint_line = piece if adjoint_line is None else adjoint_line + piece
        adjoint_ref[...] = toeplitz(adjoint_line[:edge])

    def adjoint_step(index):
        start = index * step_rows
        windows = products[:, pl.ds(start, adjoint_window), :].reshape(-1, cols)
        terms = jnp.dot(adjoint_ref[...], windows, preferred_element_type=jnp.float32)
        beside = jnp.zeros((step_rows, lanes - cols), jnp.float32)
        total = terms[radius * step_rows : (radius + 1) * step_rows, :]
        for tap in range(edge):
            if tap != radius:
                term = terms[tap * step_rows : (tap + 1) * step_rows, :]
                term = jnp.concatenate([term, beside], axis=1)
                total = total + pltpu.roll(term, (tap - radius) % lanes, 1)[:, :cols]
        out_ref[pl.ds(start, step_rows), :] = total * live_line

    lead = 2 * margin // step_rows
    for index in range(lead):
        forward_step(index)
    build_adjoint()
    for index in range(share // step_rows):
        forward_step(index + lead)
        if index:
            adjoint_step(index - 1)
    adjoint_step(share // step_rows - 1)

    @pl.when(sends_up)
    def _():
        halo_copy(0, column + 1).wait_send()

    @pl.when(sends_down)
    def _():
        halo_copy(1, column - 1).wait_send()


def on_device(theta, target, occupancy, kernels, kernel_weights):
    local_rows, cols = theta.shape
    layouts, sharers = lax.axis_size("layout"), lax.axis_size("kernel")
    own_channels = kernels.shape[0] * kernels.shape[1]
    channels = own_channels * sharers
    edge = kernels.shape[-1]
    share = local_rows // sharers
    lanes = cols + 128
    forward_window = -(-(step_rows + edge - 1) // 8) * 8
    forward_depth = -(-edge * forward_window // 128) * 128
    adjoint_window = step_rows + 2 * margin
    near_rows = share + 2 * margin
    vmem = pltpu.VMEM
    kernels = jnp.transpose(kernels, (0, 2, 1, 3))
    weights = kernel_weights.reshape(1, -1)
    return pl.pallas_call(
        functools.partial(band_kernel, layouts, sharers),
        out_shape=jax.ShapeDtypeStruct((share, cols), jnp.float32),
        in_specs=[pl.BlockSpec(memory_space=pltpu.HBM)] * 5,
        out_specs=pl.BlockSpec(memory_space=vmem),
        scratch_shapes=[
            vmem(theta.shape, theta.dtype),
            vmem(target.shape, target.dtype),
            vmem(occupancy.shape, occupancy.dtype),
            vmem(kernels.shape, kernels.dtype),
            vmem(weights.shape, weights.dtype),
            pltpu.SemaphoreType.DMA((5,)),
            vmem((sharers, tap_rows, 128), jnp.float32),
            vmem((halo_rows + 2 * margin, cols), jnp.bfloat16),
            vmem((2, halo_rows + 2 * margin, cols), jnp.bfloat16),
            vmem((share + 2 * halo_rows, lanes), jnp.float32),
            vmem((near_rows, cols), jnp.float32),
            vmem((near_rows, cols), jnp.float32),
            vmem((edge, near_rows - step_rows + forward_window, cols), jnp.float32),
            vmem((channels, near_rows, cols), jnp.bfloat16),
            vmem((channels * step_rows, forward_depth), jnp.bfloat16),
            vmem((edge * step_rows, channels * adjoint_window), jnp.bfloat16),
            pltpu.SemaphoreType.DMA((sharers,)),
            pltpu.SemaphoreType.DMA((sharers,)),
            pltpu.SemaphoreType.DMA,
            pltpu.SemaphoreType.DMA((2,)),
        ],
        compiler_params=pltpu.CompilerParams(
            collective_id=0, has_side_effects=True, vmem_limit_bytes=48 * 1024 * 1024
        ),
    )(*(pltpu.with_memory_space_constraint(x, pltpu.HBM) for x in (theta, target, occupancy, kernels, weights)))


def solution(mesh):
    placed = (
        P(("group", "layout"), None),
        P(("group", "layout"), None),
        P(("group", "layout"), None),
        P(None, "kernel", None, None),
        P("kernel"),
    )
    return jax.shard_map(
        on_device,
        mesh=mesh,
        in_specs=placed,
        out_specs=P(("group", "layout", "kernel"), None),
        check_vma=False,
    )
```

```python
import functools
import jax
import jax.numpy as jnp
from jax import lax
from jax.experimental import pallas as pl
from jax.experimental.pallas import tpu as pltpu
from jax.sharding import PartitionSpec as P

steepness = 8.0
threshold = 1.0
step_rows = 16
margin = 16
halo_rows = 32
tap_rows = 24
tap_lanes = 32
mesh_id = pl.DeviceIdType.MESH


def band_kernel(
    layouts, sharers, theta_hbm, target_hbm, occupancy_hbm, kernels_hbm, weights_hbm, out_ref,
    theta_ref, target_ref, occupancy_ref, kernels_ref, weights_ref, load_sem, gathered, halo_out, halo_in, mask_ref, target_near, live_near, shifted, windows_ref, products, forward_ref,
    adjoint_ref, send_sem, recv_sem, halo_send_sem, halo_recv_sem,
):
    local_rows, cols = theta_ref.shape
    parts, edge, own_kernels, _ = kernels_ref.shape
    own_channels = parts * own_kernels
    channels = own_channels * sharers
    radius = edge // 2
    share = local_rows // sharers
    lanes = mask_ref.shape[1]
    forward_window = (shifted.shape[1] - (share + 2 * margin)) + step_rows
    forward_depth = forward_ref.shape[1]
    adjoint_window = step_rows + 2 * margin
    adjoint_depth = adjoint_ref.shape[1]
    column = lax.axis_index("layout")
    sharer = lax.axis_index("kernel")
    is_first = sharer == 0
    is_last = sharer == sharers - 1
    has_low = jnp.logical_and(is_first, column > 0)
    has_high = jnp.logical_and(is_last, column < layouts - 1)
    sends_up = jnp.logical_and(is_first, column < layouts - 1)
    sends_down = jnp.logical_and(is_last, column > 0)
    at_edge = jnp.logical_or(is_first, is_last)

    loads = [
        pltpu.make_async_copy(source, place, load_sem.at[index])
        for index, (source, place) in enumerate((
            (kernels_hbm, kernels_ref), (weights_hbm, weights_ref),
            (occupancy_hbm, occupancy_ref), (theta_hbm, theta_ref), (target_hbm, target_ref),
        ))
    ]
    for load in loads:
        load.start()

    barrier = pltpu.get_barrier_semaphore()
    for offset in range(1, sharers):
        pl.semaphore_signal(
            barrier, inc=1, device_id={"kernel": lax.rem(sharer + offset, sharers)},
            device_id_type=mesh_id,
        )

    @pl.when(jnp.logical_and(at_edge, column > 0))
    def _():
        pl.semaphore_signal(
            barrier, inc=1, device_id={"layout": column - 1}, device_id_type=mesh_id
        )

    @pl.when(jnp.logical_and(at_edge, column < layouts - 1))
    def _():
        pl.semaphore_signal(
            barrier, inc=1, device_id={"layout": column + 1}, device_id_type=mesh_id
        )

    gathered[0] = jnp.zeros(gathered.shape[1:], jnp.float32)
    loads[0].wait()
    loads[1].wait()
    for channel in range(own_channels):
        part, own = channel // own_kernels, channel % own_kernels
        lane_start = channel * tap_lanes
        taps = kernels_ref[part].astype(jnp.float32)
        for tap in range(edge):
            gathered[0, tap : tap + 1, lane_start : lane_start + edge] = taps[tap, own : own + 1]
        gathered[0, edge : edge + 1, lane_start : lane_start + edge] = jnp.broadcast_to(
            weights_ref[0:1, own : own + 1], (1, edge)
        )
    greeted = (column > 0).astype(jnp.int32) + (column < layouts - 1).astype(jnp.int32)
    pl.semaphore_wait(barrier, sharers - 1 + at_edge.astype(jnp.int32) * greeted)

    tap_copies = [
        pltpu.make_async_remote_copy(
            src_ref=gathered.at[0], dst_ref=gathered.at[offset], send_sem=send_sem.at[offset],
            recv_sem=recv_sem.at[offset],
            device_id={"kernel": lax.rem(sharer + offset, sharers)}, device_id_type=mesh_id,
        )
        for offset in range(1, sharers)
    ]
    for copy in tap_copies:
        copy.start()

    for load in loads[2:]:
        load.wait()

    tile_edge = cols // occupancy_ref.shape[1]
    lane = lax.broadcasted_iota(jnp.int32, (1, cols), 1)
    live_line = jnp.zeros((1, cols), jnp.float32)
    for tile in range(occupancy_ref.shape[1]):
        inside = jnp.logical_and(lane >= tile * tile_edge, lane < (tile + 1) * tile_edge)
        live_line = jnp.where(inside, occupancy_ref[0:1, tile : tile + 1].astype(jnp.float32), live_line)

    def mask_of(start, count):
        values = jax.nn.sigmoid(theta_ref[pl.ds(start, count), :].astype(jnp.float32)) * live_line
        return values.astype(jnp.bfloat16)

    def fill_halo(theta_start, target_start):
        halo_out[0:halo_rows, :] = mask_of(theta_start, halo_rows)
        halo_out[halo_rows : halo_rows + margin, :] = target_ref[pl.ds(target_start, margin), :]
        halo_out[halo_rows + margin :, :] = jnp.broadcast_to(live_line, (margin, cols)).astype(
            jnp.bfloat16
        )

    @pl.when(sends_up)
    def _():
        fill_halo(local_rows - halo_rows, local_rows - margin)

    @pl.when(sends_down)
    def _():
        fill_halo(0, 0)

    def halo_copy(side, neighbour):
        return pltpu.make_async_remote_copy(
            src_ref=halo_out, dst_ref=halo_in.at[side], send_sem=halo_send_sem,
            recv_sem=halo_recv_sem.at[side], device_id={"layout": neighbour},
            device_id_type=mesh_id,
        )

    @pl.when(sends_up)
    def _():
        halo_copy(0, column + 1).start()

    @pl.when(sends_down)
    def _():
        halo_copy(1, column - 1).start()

    first = pl.multiple_of(sharer * share, 32)
    mask_ref[:, cols:] = jnp.zeros((share + 2 * halo_rows, lanes - cols), jnp.float32)
    mask_ref[halo_rows : halo_rows + share, :cols] = mask_of(first, share).astype(jnp.float32)
    target_near[margin : margin + share, :] = target_ref[pl.ds(first, share), :].astype(
        jnp.float32
    )
    live_near[margin : margin + share, :] = jnp.broadcast_to(live_line, (share, cols))

    def place(mask_at, near_at, mask_values, target_values, live_values):
        mask_ref[mask_at : mask_at + halo_rows, :cols] = mask_values
        target_near[near_at : near_at + margin, :] = target_values
        live_near[near_at : near_at + margin, :] = live_values

    def place_own(mask_at, near_at, mask_start, near_start):
        place(
            mask_at, near_at, mask_of(mask_start, halo_rows).astype(jnp.float32),
            target_ref[pl.ds(near_start, margin), :].astype(jnp.float32),
            jnp.broadcast_to(live_line, (margin, cols)),
        )

    def place_received(mask_at, near_at, side):
        place(
            mask_at, near_at, halo_in[side, 0:halo_rows, :].astype(jnp.float32),
            halo_in[side, halo_rows : halo_rows + margin, :].astype(jnp.float32),
            halo_in[side, halo_rows + margin :, :].astype(jnp.float32),
        )

    def place_nothing(mask_at, near_at):
        place(
            mask_at, near_at, jnp.zeros((halo_rows, cols), jnp.float32),
            jnp.zeros((margin, cols), jnp.float32), jnp.zeros((margin, cols), jnp.float32),
        )

    high_mask, high_near = halo_rows + share, margin + share

    @pl.when(jnp.logical_not(is_first))
    def _():
        place_own(
            0, 0, pl.multiple_of(first - halo_rows, 32), pl.multiple_of(first - margin, 16)
        )

    @pl.when(jnp.logical_not(is_last))
    def _():
        after = pl.multiple_of(first + share, 32)
        place_own(high_mask, high_near, after, after)

    @pl.when(jnp.logical_and(is_first, column == 0))
    def _():
        place_nothing(0, 0)

    @pl.when(jnp.logical_and(is_last, column == layouts - 1))
    def _():
        place_nothing(high_mask, high_near)

    spread_row = lax.broadcasted_iota(jnp.int32, (128, forward_depth), 0)
    spread_lane = lax.broadcasted_iota(jnp.int32, (128, forward_depth), 1)
    spreads = []
    for channel in range(own_channels):
        ahead = spread_lane - forward_window * (spread_row - channel * tap_lanes)
        spread = jnp.logical_and(ahead >= 0, ahead < forward_window)
        spreads.append(jnp.where(spread, 1.0, 0.0).astype(jnp.bfloat16))
    line = lax.broadcasted_iota(jnp.int32, (tap_rows, forward_depth), 1)
    down = lax.broadcasted_iota(jnp.int32, (tap_rows, forward_depth), 0)
    chosen = jnp.zeros((tap_rows, forward_depth), jnp.float32)
    for tap in range(edge):
        chosen = jnp.where(line - forward_window * tap == down, 1.0, chosen)
    chosen = jnp.where(down < edge, chosen, 0.0)
    group_depth = sharers * adjoint_window
    turn_lanes = -(-group_depth // 128) * 128
    extent = (sharers, tap_rows, turn_lanes)
    slot_at = lax.broadcasted_iota(jnp.int32, extent, 0)
    row_at = lax.broadcasted_iota(jnp.int32, extent, 1)
    lane_at = lax.broadcasted_iota(jnp.int32, extent, 2)
    turn = lane_at == slot_at * adjoint_window + (margin + radius) - row_at
    turn = jnp.logical_and(turn, row_at < edge)
    turn = jnp.where(turn, 1.0, 0.0).reshape(sharers * tap_rows, turn_lanes).astype(jnp.bfloat16)

    @pl.when(has_low)
    def _():
        halo_copy(0, column - 1).wait_recv()
        place_received(0, 0, 0)

    @pl.when(has_high)
    def _():
        halo_copy(1, column + 1).wait_recv()
        place_received(high_mask, high_near, 1)

    skip = halo_rows - margin - radius
    around = mask_ref[skip : skip + shifted.shape[1], :]
    for tap in range(edge):
        moved = around if tap == radius else pltpu.roll(around, (radius - tap) % lanes, 1)
        shifted[tap] = moved[:, :cols]
    pad_depth = forward_depth - edge * forward_window
    for index in range(windows_ref.shape[0]):
        start = index * step_rows
        windows = shifted[:, start : start + forward_window, :].reshape(-1, cols)
        windows = jnp.concatenate([windows, jnp.zeros((pad_depth, cols), jnp.float32)], axis=0)
        windows_ref[index] = windows.astype(jnp.bfloat16)

    for copy in tap_copies:
        copy.wait()

    taps = gathered[...].reshape(sharers * tap_rows, 128).astype(jnp.bfloat16)
    lines = []
    for spread in spreads:
        wide = jnp.dot(taps, spread, preferred_element_type=jnp.float32)
        wide = wide.reshape(sharers, tap_rows, forward_depth)
        lines.append(jnp.sum(wide * chosen[None], axis=1))
    forward_line = jnp.concatenate(lines, axis=0)

    def toeplitz(lines):
        count, depth = lines.shape
        rows = jnp.concatenate(
            [
                pltpu.roll(
                    jnp.broadcast_to(lines[row : row + 1], (step_rows, depth)), 0, 1, stride=1,
                    stride_axis=0,
                )
                for row in range(count)
            ],
            axis=0,
        )
        return rows.astype(jnp.bfloat16)

    forward_ref[...] = toeplitz(forward_line)

    def weight_of(channel):
        own, slot = channel // sharers, channel % sharers
        lane_start = own * tap_lanes
        return jnp.broadcast_to(
            gathered[slot, edge : edge + 1, lane_start : lane_start + 1], (step_rows, cols)
        )

    def forward_step(index):
        start = index * step_rows
        fields = jnp.dot(
            forward_ref[...], windows_ref[index], preferred_element_type=jnp.float32
        ).reshape(channels, step_rows, cols)
        intensity = jnp.zeros((step_rows, cols), jnp.float32)
        for channel in range(channels):
            intensity += weight_of(channel) * (fields[channel] * fields[channel])
        resist = jax.nn.sigmoid(steepness * (intensity - threshold))
        response = 2.0 * steepness * (resist - target_near[pl.ds(start, step_rows), :])
        response = response * resist * (1.0 - resist) * live_near[pl.ds(start, step_rows), :]
        for channel in range(channels):
            factor = 2.0 * weight_of(channel) * response
            products[channel, pl.ds(start, step_rows), :] = (factor * fields[channel]).astype(
                jnp.bfloat16
            )

    def build_adjoint():
        turned = lax.dot_general(
            taps, turn, (((0,), (0,)), ((), ())), preferred_element_type=jnp.float32
        )
        rest = jnp.zeros((tap_rows, adjoint_depth - turn_lanes), jnp.float32)
        adjoint_line = None
        for channel in range(own_channels):
            piece = turned[channel * tap_lanes : channel * tap_lanes + tap_rows]
            piece = jnp.concatenate([piece, rest], axis=1)
            if channel:
                piece = pltpu.roll(piece, channel * group_depth, 1)
            adjoint_line = piece if adjoint_line is None else adjoint_line + piece
        adjoint_ref[...] = toeplitz(adjoint_line[:edge])

    def adjoint_step(index):
        start = index * step_rows
        windows = products[:, pl.ds(start, adjoint_window), :].reshape(-1, cols)
        terms = jnp.dot(adjoint_ref[...], windows, preferred_element_type=jnp.float32)
        beside = jnp.zeros((step_rows, lanes - cols), jnp.float32)
        total = terms[radius * step_rows : (radius + 1) * step_rows, :]
        for tap in range(edge):
            if tap != radius:
                term = terms[tap * step_rows : (tap + 1) * step_rows, :]
                term = jnp.concatenate([term, beside], axis=1)
                total = total + pltpu.roll(term, (tap - radius) % lanes, 1)[:, :cols]
        out_ref[pl.ds(start, step_rows), :] = total * live_line

    lead = 2 * margin // step_rows
    for index in range(lead):
        forward_step(index)
    build_adjoint()
    for index in range(share // step_rows):
        forward_step(index + lead)
        if index:
            adjoint_step(index - 1)
    adjoint_step(share // step_rows - 1)

    @pl.when(sends_up)
    def _():
        halo_copy(0, column + 1).wait_send()

    @pl.when(sends_down)
    def _():
        halo_copy(1, column - 1).wait_send()


def on_device(theta, target, occupancy, kernels, kernel_weights):
    local_rows, cols = theta.shape
    layouts, sharers = lax.axis_size("layout"), lax.axis_size("kernel")
    own_channels = kernels.shape[0] * kernels.shape[1]
    channels = own_channels * sharers
    edge = kernels.shape[-1]
    share = local_rows // sharers
    lanes = cols + 128
    forward_window = -(-(step_rows + edge - 1) // 8) * 8
    forward_depth = -(-edge * forward_window // 128) * 128
    adjoint_window = step_rows + 2 * margin
    near_rows = share + 2 * margin
    vmem = pltpu.VMEM
    kernels = jnp.transpose(kernels, (0, 2, 1, 3))
    weights = kernel_weights.reshape(1, -1)
    return pl.pallas_call(
        functools.partial(band_kernel, layouts, sharers),
        out_shape=jax.ShapeDtypeStruct((share, cols), jnp.float32),
        in_specs=[pl.BlockSpec(memory_space=pltpu.HBM)] * 5,
        out_specs=pl.BlockSpec(memory_space=vmem),
        scratch_shapes=[
            vmem(theta.shape, theta.dtype),
            vmem(target.shape, target.dtype),
            vmem(occupancy.shape, occupancy.dtype),
            vmem(kernels.shape, kernels.dtype),
            vmem(weights.shape, weights.dtype),
            pltpu.SemaphoreType.DMA((5,)),
            vmem((sharers, tap_rows, 128), jnp.float32),
            vmem((halo_rows + 2 * margin, cols), jnp.bfloat16),
            vmem((2, halo_rows + 2 * margin, cols), jnp.bfloat16),
            vmem((share + 2 * halo_rows, lanes), jnp.float32),
            vmem((near_rows, cols), jnp.float32),
            vmem((near_rows, cols), jnp.float32),
            vmem((edge, near_rows - step_rows + forward_window, cols), jnp.float32),
            vmem((near_rows // step_rows, forward_depth, cols), jnp.bfloat16),
            vmem((channels, near_rows, cols), jnp.bfloat16),
            vmem((channels * step_rows, forward_depth), jnp.bfloat16),
            vmem((edge * step_rows, channels * adjoint_window), jnp.bfloat16),
            pltpu.SemaphoreType.DMA((sharers,)),
            pltpu.SemaphoreType.DMA((sharers,)),
            pltpu.SemaphoreType.DMA,
            pltpu.SemaphoreType.DMA((2,)),
        ],
        compiler_params=pltpu.CompilerParams(
            collective_id=0, has_side_effects=True, vmem_limit_bytes=48 * 1024 * 1024
        ),
    )(*(pltpu.with_memory_space_constraint(x, pltpu.HBM) for x in (theta, target, occupancy, kernels, weights)))


def solution(mesh):
    placed = (
        P(("group", "layout"), None),
        P(("group", "layout"), None),
        P(("group", "layout"), None),
        P(None, "kernel", None, None),
        P("kernel"),
    )
    return jax.shard_map(
        on_device,
        mesh=mesh,
        in_specs=placed,
        out_specs=P(("group", "layout", "kernel"), None),
        check_vma=False,
    )
```
